512 devices in a mesh: gx: 8 (over x, core), gy: 8 (over y), gz: 8 (over z).
Axes of the slice: x: 4, y: 8, z: 8, core: 2. Of those that a mesh axis runs over, the one named last changes fastest.
Arguments:
- right_side: float32 [96, 96, 4096], P('gx', 'gy', 'gz'), may hold values from -8 to 8
- phase: int32 [96, 96, 4096], P('gx', 'gy', 'gz'), may hold values 0 or 1
Outputs:
- correction: float32 [96, 96, 4096], P('gx', 'gy', 'gz')
- remainder: float32 [96, 96, 4096], P('gx', 'gy', 'gz')
The draws below stay inside these ranges and needn't reach their ends.
All inputs are finite; a program needn't handle non-finite values. No bound on the sum of `phase` on one device may be relied on, other than what follows from the above.
Results may differ from the reference program's by a relative error of at most 0.000067.
Values sent between devices are 32-bit elements; how exact they have to be, the bound alone decides.
A program may use at most 128 MiB of HBM per device.

```python
import jax
import jax.numpy as jnp

DEGREE = 4
COARSE_ITERS = 8
NX = 96
NY = 96
NZ = 4096


def touch_ends(entries, stream_key, low, top_value):
    dims = entries.shape
    spot = [jax.random.randint(jax.random.fold_in(stream_key, axis), (), 0, dims[axis]) for axis in range(len(dims))]
    entries = entries.at[tuple(spot)].set(low)
    longest = dims.index(max(dims))
    spot[longest] = (spot[longest] + 1) % dims[longest]
    return entries.at[tuple(spot)].set(top_value)


def block_levels(own_key, shape, pieces, least, high):
    level, own = 1.0, jax.random.fold_in(own_key, 6)
    for position, shards_of in pieces:
        steps = jnp.exp(jax.random.uniform(jax.random.fold_in(own, position), (shards_of,), jnp.float32, least / len(pieces), high / len(pieces)))
        level = level * jnp.repeat(steps, shape[position] // shards_of).reshape([-1 if axis == position else 1 for axis in range(len(shape))])
    return level


def bell_draw(stream_key, extent, scale, bound, pieces=(), dtype=jnp.bfloat16):
    result = jax.random.normal(stream_key, extent, jnp.float32) * scale
    if len(pieces) > 0:
        result = block_levels(stream_key, extent, pieces, -0.22, 0.18) * result
    return jnp.clip(result, min=-bound, max=bound).astype(dtype)


def setup_inputs(seed: int = 0) -> dict:
    seeds = jax.random.split(jax.random.key(seed), 3)
    return {
        "right_side": bell_draw(seeds[0], (NX, NY, NZ), 1.0, 8.0, ((0, 8), (1, 8), (2, 8)), jnp.float32),
        "phase": touch_ends((jax.random.randint(seeds[1], (NX, NY, NZ), 0, 3) < 1).astype(jnp.int32), jax.random.fold_in(seeds[1], 1), 0, 1),
    }


heavy_density = 20.0
smooth_lowest = 0.3
coarse_lowest = 0.02
upper_bound = 2.0


def nearby(padded):
    return [padded[2:, 1:-1, 1:-1], padded[:-2, 1:-1, 1:-1],
            padded[1:-1, 2:, 1:-1], padded[1:-1, :-2, 1:-1],
            padded[1:-1, 1:-1, 2:], padded[1:-1, 1:-1, :-2]]


def pad_zero(values):
    return jnp.pad(values, 1)


def coefficients(density, padded_density, factor):
    facing = [2.0 / (density + other) for other in nearby(padded_density)]
    total = facing[0] + facing[1] + facing[2] + facing[3] + facing[4] + facing[5]
    return facing, factor * total


def operate(values, padder, facing, diagonal, factor):
    others = nearby(padder(values))
    summed = facing[0] * others[0]
    for index in range(1, 6):
        summed = summed + facing[index] * others[index]
    return diagonal * values - factor * summed


def chebyshev(initial, residual, facing, diagonal, factor, padder, degree, lowest, finish):
    middle = (upper_bound + lowest) / 2.0
    radius = (upper_bound - lowest) / 2.0
    sharpness = middle / radius
    weight_old = 1.0 / sharpness
    inverse = 1.0 / diagonal
    direction = inverse * residual * (1.0 / middle)
    solution = initial + direction
    if finish or degree > 1:
        residual = residual - operate(direction, padder, facing, diagonal, factor)
    for sweep_index in range(1, degree):
        weight_new = 1.0 / (2.0 * sharpness - weight_old)
        direction = (weight_new * weight_old) * direction + (2.0 * weight_new / radius) * (inverse * residual)
        solution = solution + direction
        if finish or sweep_index < degree - 1:
            residual = residual - operate(direction, padder, facing, diagonal, factor)
        weight_old = weight_new
    return solution, residual


def restrict(values):
    sizes = values.shape
    grouped = values.reshape(sizes[0] // 2, 2, sizes[1] // 2, 2, sizes[2] // 2, 2)
    return jnp.mean(grouped, axis=(1, 3, 5))


def prolong(values):
    return jnp.repeat(jnp.repeat(jnp.repeat(values, 2, 0), 2, 1), 2, 2)


def reference(right_side, phase):
    density0 = jnp.where(phase == 1, heavy_density, 1.0).astype(jnp.float32)
    facing0, diagonal0 = coefficients(density0, pad_zero(density0), 1.0)
    x_first, r_first = chebyshev(jnp.zeros_like(right_side), right_side, facing0, diagonal0, 1.0, pad_zero, DEGREE, smooth_lowest, True)
    density1 = restrict(density0)
    facing1, diagonal1 = coefficients(density1, pad_zero(density1), 0.25)
    rhs_second = restrict(r_first)
    x_second, r_second = chebyshev(jnp.zeros_like(rhs_second), rhs_second, facing1, diagonal1, 0.25, pad_zero, DEGREE, smooth_lowest, True)
    density2 = restrict(density1)
    facing2, diagonal2 = coefficients(density2, pad_zero(density2), 0.0625)
    rhs_third = restrict(r_second)
    coarse_error, unused = chebyshev(jnp.zeros_like(rhs_third), rhs_third, facing2, diagonal2, 0.0625, pad_zero, COARSE_ITERS, coarse_lowest, False)
    lifted = prolong(coarse_error)
    x_second = x_second + lifted
    r_second = r_second - operate(lifted, pad_zero, facing1, diagonal1, 0.25)
    x_second, r_second = chebyshev(x_second, r_second, facing1, diagonal1, 0.25, pad_zero, DEGREE, smooth_lowest, True)
    lifted = prolong(x_second)
    x_first = x_first + lifted
    r_first = r_first - operate(lifted, pad_zero, facing0, diagonal0, 1.0)
    x_first, r_first = chebyshev(x_first, r_first, facing0, diagonal0, 1.0, pad_zero, DEGREE, smooth_lowest, True)
    return x_first, r_first
```

```python
import functools

import jax
import jax.numpy as jnp
from jax import lax
from jax.experimental import pallas as pl
from jax.experimental.pallas import tpu as pltpu
from jax.sharding import PartitionSpec as P

MESH = pl.DeviceIdType.MESH
DEGREE = 4
COARSE_ITERS = 8
HEAVY = 20.0
SMOOTH_LOWEST = 0.3
COARSE_LOWEST = 0.02
UPPER = 2.0

LEVELS = (
    dict(n=12, h=6, t=5, cols=24, rows=32),
    dict(n=6, h=8, t=3, cols=22, rows=32),
    dict(n=3, h=8, t=2, cols=19, rows=32),
)


def weights(lowest, degree):
    middle, radius = (UPPER + lowest) / 2.0, (UPPER - lowest) / 2.0
    sharpness = middle / radius
    old = 1.0 / sharpness
    pairs = []
    for _ in range(1, degree):
        new = 1.0 / (2.0 * sharpness - old)
        pairs.append((new * old, 2.0 * new / radius))
        old = new
    return 1.0 / middle, pairs


def columns(lo, hi, unroll, body, carry):
    trips = (hi - lo) // unroll

    def several(k, c):
        for j in range(unroll):
            c = body(lo + k * unroll + j, c)
        return c

    if trips > 1:
        carry = lax.fori_loop(0, trips, several, carry)
    elif trips == 1:
        carry = several(0, carry)
    for i in range(lo + trips * unroll, hi):
        carry = body(i, carry)
    return carry


def lanes(shape):
    return lax.broadcasted_iota(jnp.int32, shape, len(shape) - 1)


def shifted(blocks, towards):
    count = len(blocks)
    shape = blocks[0].shape
    edge = lanes(shape) == (127 if towards > 0 else 0)
    rolled = [pltpu.roll(v, 127 if towards > 0 else 1, 1) for v in blocks]
    return [jnp.where(edge, rolled[(t + towards) % count], rolled[t]) for t in range(count)]


def split(block):
    return [block[t] for t in range(block.shape[0])]


def picked(value, index):
    return jnp.take_along_axis(value, index, axis=1)


def halved(blocks):
    lane = lanes(blocks[0].shape)
    index = (2 * lane) % 128
    pairs = [picked(v + pltpu.roll(v, 127, 1), index) for v in blocks]
    out = [jnp.where(lane < 64, pairs[2 * t], pairs[2 * t + 1]) for t in range(len(blocks) // 2)]
    out.append(pairs[-1])
    return out


def doubled(blocks):
    lane = lanes(blocks[0].shape)
    low, high = lane // 2, 64 + lane // 2
    out = []
    for v in blocks[:-1]:
        out += [picked(v, low), picked(v, high)]
    out.append(picked(blocks[-1], jnp.where(lane < 64, low, high)))
    return out


def reach(offset, n, w):
    return max(offset * n, -w), min(offset * n + n, n + w)


class Sender:
    def __init__(self, send_sems, recv_sems, sizes):
        self.send, self.recv, self.used = send_sems, recv_sems, 0
        self.sizes = sizes
        self.pending = []

    def target(self, offset):
        place = []
        for axis, o in zip(("gx", "gy", "gz"), offset):
            size = self.sizes[axis]
            place.append(lax.rem(lax.axis_index(axis) + (o + 4 * size), size) if o else lax.axis_index(axis))
        return tuple(place)

    def start(self, src, dst, offset):
        copy = pltpu.make_async_remote_copy(
            src_ref=src,
            dst_ref=dst,
            send_sem=self.send.at[self.used],
            recv_sem=self.recv.at[self.used],
            device_id=self.target(offset),
            device_id_type=MESH,
        )
        copy.start()
        self.used += 1
        return copy

    def exchange(self, ref, level, w, offsets, tiles=None, whole_y=False):
        n, h = level["n"], level["h"]
        t0, t1 = tiles or (0, level["t"])
        copies = []
        for ox, oy in offsets:
            x0, x1 = reach(ox, n, w)
            if whole_y:
                y0, y1 = -w, n + w
            else:
                y0, y1 = reach(oy, n, w)
            sx, sy = x0 - ox * n + h, y0 - oy * n + h
            copies.append(
                self.start(
                    ref.at[sx : sx + x1 - x0, t0:t1, sy : sy + y1 - y0, :],
                    ref.at[x0 + h : x1 + h, t0:t1, y0 + h : y1 + h, :],
                    (-ox, -oy, 0),
                )
            )
        return copies


def wait_recv(copies):
    for copy in copies:
        copy.wait_recv()


def wait_send(copies):
    for copy in copies:
        copy.wait_send()


def near(o, n):
    return (abs(o) - 1) * n + 1 if o else 0


def diamond(n, w, most):
    found = []
    for ox in range(-most, most + 1):
        for oy in range(-most, most + 1):
            if (ox or oy) and near(ox, n) + near(oy, n) <= w:
                found.append((ox, oy))
    return sorted(found, key=lambda o: -abs(o[0]) - abs(o[1]))


AROUND = diamond(1, 2, 1)


def clear_outside(ref, level, w, sizes):
    n, h, t = level["n"], level["h"], level["t"]

    def clear(x0, x1, y0, y1):
        zero = jnp.zeros((t, y1 - y0, 128), jnp.float32)

        def body(i, c):
            ref[i, :, y0:y1, :] = zero
            return c

        lax.fori_loop(x0, x1, body, 0)

    gx, gy = lax.axis_index("gx"), lax.axis_index("gy")
    for k in range(-(-w // n)):
        below, above = (h - w, h - k * n), (h + n + k * n, h + n + w)
        every = (h - w, h + n + w)
        pl.when(gx == k)(functools.partial(clear, *below, *every))
        pl.when(gx == sizes["gx"] - 1 - k)(functools.partial(clear, *above, *every))
        pl.when(gy == k)(functools.partial(clear, *every, *below))
        pl.when(gy == sizes["gy"] - 1 - k)(functools.partial(clear, *every, *above))


def conduct(a, b, scale):
    return scale / jnp.maximum(a + b, 0.5)


def coefficients(rho, co, level, w, scale, unroll, first=None):
    bx, by, bzp, bzm, iv = co
    n, h = level["n"], level["h"]
    lo, hi, rows = h - w, h + n + w, n + 2 * w
    ys = pl.ds(lo, rows)

    def body(i, before):
        here = rho[i, :, ys, :]
        after = conduct(here, rho[i + 1, :, ys, :], scale)
        bx[i, :, ys, :] = after
        by[i, :, pl.ds(lo - 1, rows + 1), :] = conduct(
            rho[i, :, pl.ds(lo - 1, rows + 1), :], rho[i, :, pl.ds(lo, rows + 1), :], scale
        )
        above = jnp.stack([conduct(a, b, scale) for a, b in zip(split(here), shifted(split(here), 1))])
        below = jnp.stack(shifted(split(above), -1))
        bzp[i, :, ys, :] = above
        bzm[i, :, ys, :] = below
        total = (before + after) + (above + below) + (by[i, :, ys, :] + by[i, :, pl.ds(lo - 1, rows), :])
        inverse = jnp.where(here > 0.0, 1.0 / total, 0.0)
        iv[i, :, ys, :] = inverse
        if first is not None:
            r, d, weight = first
            d[i, :, ys, :] = weight * (inverse * r[i, :, ys, :])
        return after

    start = conduct(rho[lo - 1, :, ys, :], rho[lo, :, ys, :], scale)
    bx[lo - 1, :, ys, :] = start
    columns(lo, hi, unroll, body, start)


def begin(r, iv, d, level, w, weight, unroll):
    n, h = level["n"], level["h"]
    ys = pl.ds(h - w, n + 2 * w)

    def body(i, c):
        d[i, :, ys, :] = weight * (iv[i, :, ys, :] * r[i, :, ys, :])
        return c

    columns(h - w, h + n + w, unroll, body, 0)


def sweep(v, co, level, w, unroll, finish, tiles=None):
    bx, by, bzp, bzm, _ = co
    n, h, t = level["n"], level["h"], level["t"]
    lo, hi, rows = h - w, h + n + w, n + 2 * w
    ys, up, down = pl.ds(lo, rows), pl.ds(lo + 1, rows), pl.ds(lo - 1, rows)

    def body(i, carry):
        here, before = carry
        after = v[i + 1, :, ys, :]
        flux = bx[i, :, ys, :] * (here - after)
        parts = split(here)
        zp = jnp.stack(shifted(parts, 1))
        zm = jnp.stack(shifted(parts, -1))
        total = (flux - before) + bzp[i, :, ys, :] * (here - zp) + bzm[i, :, ys, :] * (here - zm)
        total = total + by[i, :, ys, :] * (here - v[i, :, up, :])
        total = total + by[i, :, down, :] * (here - v[i, :, down, :])
        finish(i, ys, here, total)
        return after, flux

    here = v[lo, :, ys, :]
    before = bx[lo - 1, :, ys, :] * (v[lo - 1, :, ys, :] - here)
    columns(lo, hi, unroll, body, (here, before))


def smooth(v, r, d, co, level, w, alpha, beta, unroll, total=None):
    iv = co[4]

    def finish(i, ys, here, applied):
        rest = r[i, :, ys, :] - applied
        r[i, :, ys, :] = rest
        new = beta * (iv[i, :, ys, :] * rest)
        if alpha is not None:
            new = alpha * here + new
        d[i, :, ys, :] = new
        if total is not None:
            total[i, :, ys, :] = total[i, :, ys, :] + new

    sweep(v, co, level, w, unroll, finish)


def restricted(fine, coarse, level_fine, level_coarse):
    h, n, hc = level_fine["h"], level_coarse["n"], level_coarse["h"]

    def body(i, c):
        x = h + 2 * i
        even, odd = pl.ds(h, n, stride=2), pl.ds(h + 1, n, stride=2)
        blocks = []
        for t in range(level_fine["t"]):
            both = fine[x, t, even, :] + fine[x, t, odd, :]
            both = both + (fine[x + 1, t, even, :] + fine[x + 1, t, odd, :])
            blocks.append(both)
        coarse[hc + i, :, hc : hc + n, :] = jnp.stack(halved(blocks)) * 0.125
        return c

    for i in range(n):
        body(i, 0)


def prolonged(coarse, fine, level_coarse, level_fine, w):
    hc, h, n = level_coarse["h"], level_fine["h"], level_coarse["n"]
    count = n + 2 * w

    def body(k, c):
        block = doubled(split(coarse[hc - w + k, :, hc - w : hc - w + count, :]))
        for t, v in enumerate(block):
            for x in (0, 1):
                for y in (0, 1):
                    fine[h - 2 * w + 2 * k + x, t, pl.ds(h - 2 * w + y, count, stride=2), :] = v
        return c

    columns(0, count, 3, body, 0)


def kernel(sizes, rhs, phase, out_x, out_r, *scratch):
    scratch = list(scratch)

    def take(count):
        taken, scratch[:count] = scratch[:count], []
        return taken

    rho0, r0, up0, u0, x0, d01, d02, d03, d04 = take(9)
    co0 = take(5)
    rho1, r1, up1, u1, x1, d11, d12, d13, d14 = take(9)
    co1 = take(5)
    rho2, r2, x2, d21, d22 = take(5)
    co2 = take(5)
    zs_up, zs_down, zr_below, zr_above, send_sems, recv_sems = take(6)
    l0, l1, l2 = LEVELS
    sender = Sender(send_sems, recv_sems, sizes)
    first, pairs = weights(SMOOTH_LOWEST, DEGREE)
    first2, pairs2 = weights(COARSE_LOWEST, COARSE_ITERS)

    coarse_offsets = diamond(3, 7, 3)
    line = [(o, 0) for o in (3, -3, 2, -2)] + [(0, o) for o in (3, -3, 2, -2)]
    met = {(ox, oy, 0) for ox, oy in coarse_offsets + line + AROUND} | {(0, 0, 1), (0, 0, -1)}
    barrier = pltpu.get_barrier_semaphore()
    for offset in sorted(met):
        pl.semaphore_signal(barrier, inc=1, device_id=sender.target(offset), device_id_type=MESH)

    lane = lanes((12, 128))
    own = slice(l0["h"], l0["h"] + 12)

    def prepare(i, c):
        blocks = []
        for t in range(4):
            part = slice(128 * t, 128 * t + 128)
            value = rhs[i, :, part]
            density = jnp.where(phase[i, :, part] == 1, HEAVY, 1.0).astype(jnp.float32)
            r0[i + l0["h"], t, own, :] = value
            rho0[i + l0["h"], t, own, :] = density
            blocks.append((value, density))
        zs_up[i, :12, :] = jnp.where(lane >= 64, blocks[3][0], pltpu.roll(blocks[3][1], 64, 1))
        zs_down[i, :12, :] = jnp.where(lane < 64, blocks[0][0], pltpu.roll(blocks[0][1], 64, 1))
        return c

    columns(0, 12, 4, prepare, 0)
    pl.semaphore_wait(barrier, len(met))

    along_z = [
        sender.start(zs_up.at[:, :12, :], zr_below.at[:, :12, :], (0, 0, 1)),
        sender.start(zs_down.at[:, :12, :], zr_above.at[:, :12, :], (0, 0, -1)),
    ]
    fine = sender.exchange(rho0, l0, 5, AROUND, (0, 4))
    fine += sender.exchange(r0, l0, 4, AROUND, (0, 4))

    wait_recv(along_z)
    gz = lax.axis_index("gz")
    inside = jnp.where(lane < 64, jnp.where(gz == sizes["gz"] - 1, 0.0, 1.0), jnp.where(gz == 0, 0.0, 1.0))

    def ends(i, c):
        below, above = zr_below[i, :12, :], zr_above[i, :12, :]
        r0[i + l0["h"], 4, own, :] = jnp.where(lane < 64, above, below)
        rho0[i + l0["h"], 4, own, :] = inside * pltpu.roll(jnp.where(lane < 64, below, above), 64, 1)
        return c

    columns(0, 12, 6, ends, 0)
    fine += sender.exchange(rho0, l0, 5, AROUND, (4, 5))
    fine += sender.exchange(r0, l0, 4, AROUND, (4, 5))

    restricted(rho0, rho1, l0, l1)
    restricted(rho1, rho2, l1, l2)
    line_y1, line_y2 = [(0, o) for o in (2, -2, 1, -1)], [(0, o) for o in (3, -3, 2, -2, 1, -1)]
    line_x1, line_x2 = [(o, 0) for _, o in line_y1], [(o, 0) for _, o in line_y2]
    density_y = sender.exchange(rho1, l1, 7, line_y1) + sender.exchange(rho2, l2, 8, line_y2)

    wait_recv(fine)
    wait_send(fine)
    clear_outside(rho0, l0, 5, sizes)
    coefficients(rho0, co0, l0, 4, 2.0, 1, (r0, d01, first))
    wait_recv(density_y)
    density_x = sender.exchange(rho1, l1, 7, line_x1, whole_y=True)
    density_x += sender.exchange(rho2, l2, 8, line_x2, whole_y=True)
    smooth(d01, r0, d02, co0, l0, 3, *pairs[0], 3)
    smooth(d02, r0, d03, co0, l0, 2, *pairs[1], 4)
    smooth(d03, r0, d04, co0, l0, 1, *pairs[2], 4)

    def finish_down0(i, ys, here, applied):
        up0[i, :, ys, :] = r0[i, :, ys, :] - applied
        x0[i, :, ys, :] = (d01[i, :, ys, :] + d02[i, :, ys, :]) + (d03[i, :, ys, :] + here)

    sweep(d04, co0, l0, 0, 4, finish_down0)

    restricted(up0, r1, l0, l1)
    second = sender.exchange(r1, l1, 4, AROUND)
    back0 = sender.exchange(up0, l0, 4, AROUND)
    wait_recv(density_x)
    wait_send(density_y)
    wait_send(density_x)
    clear_outside(rho1, l1, 7, sizes)
    clear_outside(rho2, l2, 8, sizes)
    coefficients(rho1, co1, l1, 6, 0.5, 2)
    coefficients(rho2, co2, l2, 7, 0.125, 2)
    wait_recv(second)
    wait_send(second)
    begin(r1, co1[4], d11, l1, 4, first, 7)
    smooth(d11, r1, d12, co1, l1, 3, *pairs[0], 6)
    smooth(d12, r1, d13, co1, l1, 2, *pairs[1], 5)
    smooth(d13, r1, d14, co1, l1, 1, *pairs[2], 8)

    def finish_down1(i, ys, here, applied):
        up1[i, :, ys, :] = r1[i, :, ys, :] - applied
        x1[i, :, ys, :] = (d11[i, :, ys, :] + d12[i, :, ys, :]) + (d13[i, :, ys, :] + here)

    sweep(d14, co1, l1, 0, 6, finish_down1)

    restricted(up1, r2, l1, l2)
    third = sender.exchange(r2, l2, 7, coarse_offsets)
    back1 = sender.exchange(up1, l1, 6, AROUND) + sender.exchange(x1, l1, 3, AROUND)
    wait_recv(third)
    wait_send(third)
    begin(r2, co2[4], d21, l2, 7, first2, 17)

    def copy_total(i, c):
        x2[i, :, l2["h"] : l2["h"] + 3, :] = d21[i, :, l2["h"] : l2["h"] + 3, :]
        return c

    columns(l2["h"], l2["h"] + 3, 3, copy_total, 0)
    v, d = d21, d22
    for k, (alpha, beta) in enumerate(pairs2):
        smooth(v, r2, d, co2, l2, 6 - k, alpha, beta, 8)
        v, d = d, v

        def add_total(i, c, v=v):
            x2[i, :, l2["h"] : l2["h"] + 3, :] = x2[i, :, l2["h"] : l2["h"] + 3, :] + v[i, :, l2["h"] : l2["h"] + 3, :]
            return c

        columns(l2["h"], l2["h"] + 3, 3, add_total, 0)

    fourth = sender.exchange(x2, l2, 4, diamond(3, 4, 2))
    wait_recv(back1)
    wait_send(back1)
    wait_recv(fourth)
    clear_outside(x2, l2, 4, sizes)
    prolonged(x2, u1, l2, l1, 4)
    smooth(u1, up1, d11, co1, l1, 6, None, first, 6)
    smooth(d11, up1, d12, co1, l1, 5, *pairs[0], 8)
    smooth(d12, up1, d13, co1, l1, 4, *pairs[1], 7)
    smooth(d13, up1, d14, co1, l1, 3, *pairs[2], 6)
    reach1 = pl.ds(l1["h"] - 3, 12)

    def finish_up1(i, c):
        total = (x1[i, :, reach1, :] + u1[i, :, reach1, :]) + (d11[i, :, reach1, :] + d12[i, :, reach1, :])
        x1[i, :, reach1, :] = total + (d13[i, :, reach1, :] + d14[i, :, reach1, :])
        return c

    columns(l1["h"] - 3, l1["h"] + 9, 6, finish_up1, 0)
    clear_outside(x1, l1, 3, sizes)

    prolonged(x1, u0, l1, l0, 3)
    wait_recv(back0)
    wait_send(back0)
    smooth(u0, up0, d01, co0, l0, 4, None, first, 3)
    smooth(d01, up0, d02, co0, l0, 3, *pairs[0], 3)
    smooth(d02, up0, d03, co0, l0, 2, *pairs[1], 4)
    smooth(d03, up0, d04, co0, l0, 1, *pairs[2], 4)

    def finish_up0(i, ys, here, applied):
        j = i - l0["h"]
        total = (x0[i, :, ys, :] + u0[i, :, ys, :]) + (d01[i, :, ys, :] + d02[i, :, ys, :])
        total = total + (d03[i, :, ys, :] + here)
        rest = up0[i, :, ys, :] - applied
        for t in range(4):
            out_x[j, :, 128 * t : 128 * t + 128] = total[t]
            out_r[j, :, 128 * t : 128 * t + 128] = rest[t]

    sweep(d04, co0, l0, 0, 4, finish_up0)
    wait_send(along_z)
    wait_send(fourth)


COPIES = 2 + 32 + 20 + 8 + 8 + 24 + 16 + 12


def per_device(sizes, right_side, phase):
    def field(level):
        return pltpu.VMEM((level["cols"], level["t"], level["rows"], 128), jnp.float32)

    l0, l1, l2 = LEVELS
    shape = jax.ShapeDtypeStruct(right_side.shape, jnp.float32)
    whole = pl.BlockSpec(memory_space=pltpu.VMEM)
    return pl.pallas_call(
        functools.partial(kernel, sizes),
        out_shape=(shape, shape),
        in_specs=[whole, whole],
        out_specs=(whole, whole),
        scratch_shapes=[field(l0)] * 14
        + [field(l1)] * 14
        + [field(l2)] * 10
        + [pltpu.VMEM((12, 16, 128), jnp.float32)] * 4
        + [pltpu.SemaphoreType.DMA((COPIES,))] * 2,
        compiler_params=pltpu.CompilerParams(
            collective_id=0, has_side_effects=True, vmem_limit_bytes=56 * 1024 * 1024
        ),
        cost_estimate=pl.CostEstimate(flops=60_000_000, bytes_accessed=1_200_000, transcendentals=0),
        name="cycle",
    )(right_side, phase)


def solution(mesh):
    spec = P("gx", "gy", "gz")
    return jax.shard_map(
        functools.partial(per_device, dict(mesh.shape)),
        mesh=mesh,
        in_specs=(spec, spec),
        out_specs=(spec, spec),
        check_vma=False,
    )
```

```python
import functools

import jax
import jax.numpy as jnp
from jax import lax
from jax.experimental import pallas as pl
from jax.experimental.pallas import tpu as pltpu
from jax.sharding import PartitionSpec as P

MESH = pl.DeviceIdType.MESH
DEGREE = 4
COARSE_ITERS = 8
HEAVY = 20.0
SMOOTH_LOWEST = 0.3
COARSE_LOWEST = 0.02
UPPER = 2.0

LEVELS = (
    dict(n=12, h=6, t=5, cols=24, rows=32),
    dict(n=6, h=8, t=3, cols=22, rows=32),
    dict(n=3, h=8, t=2, cols=19, rows=32),
)


def weights(lowest, degree):
    middle, radius = (UPPER + lowest) / 2.0, (UPPER - lowest) / 2.0
    sharpness = middle / radius
    old = 1.0 / sharpness
    pairs = []
    for _ in range(1, degree):
        new = 1.0 / (2.0 * sharpness - old)
        pairs.append((new * old, 2.0 * new / radius))
        old = new
    return 1.0 / middle, pairs


def columns(lo, hi, unroll, body, carry):
    trips = (hi - lo) // unroll

    def several(k, c):
        for j in range(unroll):
            c = body(lo + k * unroll + j, c)
        return c

    if trips > 1:
        carry = lax.fori_loop(0, trips, several, carry)
    elif trips == 1:
        carry = several(0, carry)
    for i in range(lo + trips * unroll, hi):
        carry = body(i, carry)
    return carry


def lanes(shape):
    return lax.broadcasted_iota(jnp.int32, shape, len(shape) - 1)


def shifted(blocks, towards):
    count = len(blocks)
    shape = blocks[0].shape
    edge = lanes(shape) == (127 if towards > 0 else 0)
    rolled = [pltpu.roll(v, 127 if towards > 0 else 1, 1) for v in blocks]
    return [jnp.where(edge, rolled[(t + towards) % count], rolled[t]) for t in range(count)]


def split(block):
    return [block[t] for t in range(block.shape[0])]


def picked(value, index):
    return jnp.take_along_axis(value, index, axis=1)


def halved(blocks):
    lane = lanes(blocks[0].shape)
    index = (2 * lane) % 128
    pairs = [picked(v + pltpu.roll(v, 127, 1), index) for v in blocks]
    out = [jnp.where(lane < 64, pairs[2 * t], pairs[2 * t + 1]) for t in range(len(blocks) // 2)]
    out.append(pairs[-1])
    return out


def doubled(blocks):
    lane = lanes(blocks[0].shape)
    low, high = lane // 2, 64 + lane // 2
    out = []
    for v in blocks[:-1]:
        out += [picked(v, low), picked(v, high)]
    out.append(picked(blocks[-1], jnp.where(lane < 64, low, high)))
    return out


def near(o, n):
    return (abs(o) - 1) * n + 1 if o else 0


def reach(offset, n, w):
    return max(offset * n, -w), min(offset * n + n, n + w)


class Sender:
    def __init__(self, send_sems, recv_sems, sizes):
        self.send, self.recv, self.used = send_sems, recv_sems, 0
        self.sizes = sizes
        self.pending = []

    def target(self, offset):
        place = []
        for axis, o in zip(("gx", "gy", "gz"), offset):
            size = self.sizes[axis]
            place.append(lax.rem(lax.axis_index(axis) + (o + 4 * size), size) if o else lax.axis_index(axis))
        return tuple(place)

    def start(self, src, dst, offset):
        copy = pltpu.make_async_remote_copy(
            src_ref=src,
            dst_ref=dst,
            send_sem=self.send.at[self.used],
            recv_sem=self.recv.at[self.used],
            device_id=self.target(offset),
            device_id_type=MESH,
        )
        copy.start()
        self.used += 1
        return copy

    def exchange(self, ref, level, w, offsets, tiles=None, whole_y=False):
        n, h = level["n"], level["h"]
        t0, t1 = tiles or (0, level["t"])
        copies = []
        for ox, oy in offsets:
            x0, x1 = reach(ox, n, w - near(oy, n))
            y0, y1 = (-w, n + w) if whole_y else reach(oy, n, w - near(ox, n))
            sx, sy = x0 - ox * n + h, y0 - oy * n + h
            copies.append(
                self.start(
                    ref.at[sx : sx + x1 - x0, t0:t1, sy : sy + y1 - y0, :],
                    ref.at[x0 + h : x1 + h, t0:t1, y0 + h : y1 + h, :],
                    (-ox, -oy, 0),
                )
            )
        return copies


def wait_recv(copies):
    for copy in copies:
        copy.wait_recv()


def wait_send(copies):
    for copy in copies:
        copy.wait_send()


def diamond(n, w, most):
    found = []
    for ox in range(-most, most + 1):
        for oy in range(-most, most + 1):
            if (ox or oy) and near(ox, n) + near(oy, n) <= w:
                found.append((ox, oy))
    return sorted(found, key=lambda o: -abs(o[0]) - abs(o[1]))


AROUND = diamond(1, 2, 1)


def clear_outside(ref, level, w, sizes):
    n, h, t = level["n"], level["h"], level["t"]

    def clear(x0, x1, y0, y1):
        zero = jnp.zeros((t, y1 - y0, 128), jnp.float32)

        def body(i, c):
            ref[i, :, y0:y1, :] = zero
            return c

        lax.fori_loop(x0, x1, body, 0)

    gx, gy = lax.axis_index("gx"), lax.axis_index("gy")
    for k in range(-(-w // n)):
        below, above = (h - w, h - k * n), (h + n + k * n, h + n + w)
        every = (h - w, h + n + w)
        pl.when(gx == k)(functools.partial(clear, *below, *every))
        pl.when(gx == sizes["gx"] - 1 - k)(functools.partial(clear, *above, *every))
        pl.when(gy == k)(functools.partial(clear, *every, *below))
        pl.when(gy == sizes["gy"] - 1 - k)(functools.partial(clear, *every, *above))


def conduct(a, b, scale):
    return scale / jnp.maximum(a + b, 0.5)


def coefficients(rho, co, level, w, scale, unroll):
    bx, by, bzp, bzm, iv = co
    n, h = level["n"], level["h"]
    lo, hi, rows = h - w, h + n + w, n + 2 * w
    ys = pl.ds(lo, rows)

    def body(i, before):
        here = rho[i, :, ys, :]
        after = conduct(here, rho[i + 1, :, ys, :], scale)
        bx[i, :, ys, :] = after
        by[i, :, pl.ds(lo - 1, rows + 1), :] = conduct(
            rho[i, :, pl.ds(lo - 1, rows + 1), :], rho[i, :, pl.ds(lo, rows + 1), :], scale
        )
        above = jnp.stack([conduct(a, b, scale) for a, b in zip(split(here), shifted(split(here), 1))])
        below = jnp.stack(shifted(split(above), -1))
        bzp[i, :, ys, :] = above
        bzm[i, :, ys, :] = below
        total = (before + after) + (above + below) + (by[i, :, ys, :] + by[i, :, pl.ds(lo - 1, rows), :])
        inverse = jnp.where(here > 0.0, 1.0 / total, 0.0)
        iv[i, :, ys, :] = inverse
        return after

    start = conduct(rho[lo - 1, :, ys, :], rho[lo, :, ys, :], scale)
    bx[lo - 1, :, ys, :] = start
    columns(lo, hi, unroll, body, start)


def begin(r, iv, d, level, w, weight, unroll):
    n, h = level["n"], level["h"]
    ys = pl.ds(h - w, n + 2 * w)

    def body(i, c):
        d[i, :, ys, :] = weight * (iv[i, :, ys, :] * r[i, :, ys, :])
        return c

    columns(h - w, h + n + w, unroll, body, 0)


def sweep(v, co, level, w, unroll, finish, tiles=None):
    bx, by, bzp, bzm, _ = co
    n, h, t = level["n"], level["h"], level["t"]
    lo, hi, rows = h - w, h + n + w, n + 2 * w
    ys, up, down = pl.ds(lo, rows), pl.ds(lo + 1, rows), pl.ds(lo - 1, rows)

    def body(i, carry):
        here, before = carry
        after = v[i + 1, :, ys, :]
        flux = bx[i, :, ys, :] * (here - after)
        parts = split(here)
        zp = jnp.stack(shifted(parts, 1))
        zm = jnp.stack(shifted(parts, -1))
        total = (flux - before) + bzp[i, :, ys, :] * (here - zp) + bzm[i, :, ys, :] * (here - zm)
        total = total + by[i, :, ys, :] * (here - v[i, :, up, :])
        total = total + by[i, :, down, :] * (here - v[i, :, down, :])
        finish(i, ys, here, total)
        return after, flux

    here = v[lo, :, ys, :]
    before = bx[lo - 1, :, ys, :] * (v[lo - 1, :, ys, :] - here)
    columns(lo, hi, unroll, body, (here, before))


def smooth(v, r, d, co, level, w, alpha, beta, unroll, total=None):
    iv = co[4]

    def finish(i, ys, here, applied):
        rest = r[i, :, ys, :] - applied
        r[i, :, ys, :] = rest
        new = beta * (iv[i, :, ys, :] * rest)
        if alpha is not None:
            new = alpha * here + new
        d[i, :, ys, :] = new
        if total is not None:
            total[i, :, ys, :] = total[i, :, ys, :] + new

    sweep(v, co, level, w, unroll, finish)


def restricted(fine, coarse, level_fine, level_coarse):
    h, n, hc = level_fine["h"], level_coarse["n"], level_coarse["h"]

    def body(i, c):
        x = h + 2 * i
        even, odd = pl.ds(h, n, stride=2), pl.ds(h + 1, n, stride=2)
        blocks = []
        for t in range(level_fine["t"]):
            both = fine[x, t, even, :] + fine[x, t, odd, :]
            both = both + (fine[x + 1, t, even, :] + fine[x + 1, t, odd, :])
            blocks.append(both)
        coarse[hc + i, :, hc : hc + n, :] = jnp.stack(halved(blocks)) * 0.125
        return c

    for i in range(n):
        body(i, 0)


def prolonged(coarse, fine, level_coarse, level_fine, w):
    hc, h, n = level_coarse["h"], level_fine["h"], level_coarse["n"]
    count = n + 2 * w

    def body(k, c):
        block = doubled(split(coarse[hc - w + k, :, hc - w : hc - w + count, :]))
        for t, v in enumerate(block):
            for x in (0, 1):
                for y in (0, 1):
                    fine[h - 2 * w + 2 * k + x, t, pl.ds(h - 2 * w + y, count, stride=2), :] = v
        return c

    columns(0, count, 3, body, 0)


def kernel(sizes, rhs, phase, out_x, out_r, *scratch):
    scratch = list(scratch)

    def take(count):
        taken, scratch[:count] = scratch[:count], []
        return taken

    rho0, r0, up0, u0, x0, d01, d02, d03, d04 = take(9)
    co0 = take(5)
    rho1, r1, up1, u1, x1, d11, d12, d13, d14 = take(9)
    co1 = take(5)
    rho2, r2, x2, d21, d22 = take(5)
    co2 = take(5)
    kind, zs_up, zs_down, zr_below, zr_above, local_sems, send_sems, recv_sems = take(8)
    l0, l1, l2 = LEVELS
    sender = Sender(send_sems, recv_sems, sizes)
    first, pairs = weights(SMOOTH_LOWEST, DEGREE)
    first2, pairs2 = weights(COARSE_LOWEST, COARSE_ITERS)
    own = slice(l0["h"], l0["h"] + 12)

    loads = [pltpu.make_async_copy(phase, kind, local_sems.at[4])]
    for t in range(4):
        loads.append(
            pltpu.make_async_copy(rhs.at[:, :, 128 * t : 128 * t + 128], r0.at[own, t, own, :], local_sems.at[t])
        )
    for copy in loads:
        copy.start()

    coarse_offsets = diamond(3, 7, 3)
    line_y2 = [(0, o) for o in (3, -3, 2, -2, 1, -1)]
    line_x2 = [(o, 0) for _, o in line_y2]
    met = {(ox, oy, 0) for ox, oy in coarse_offsets + line_y2 + line_x2 + AROUND} | {(0, 0, 1), (0, 0, -1)}
    barrier = pltpu.get_barrier_semaphore()
    for offset in sorted(met):
        pl.semaphore_signal(barrier, inc=1, device_id=sender.target(offset), device_id_type=MESH)

    lane = lanes((12, 128))
    for copy in loads:
        copy.wait()

    def prepare(i, c):
        x = i + l0["h"]
        density = []
        for t in range(4):
            part = slice(128 * t, 128 * t + 128)
            density.append(jnp.where(kind[i, :, part] == 1, HEAVY, 1.0).astype(jnp.float32))
            rho0[x, t, own, :] = density[t]
        zs_up[i, :12, :] = jnp.where(lane >= 64, r0[x, 3, own, :], pltpu.roll(density[3], 64, 1))
        zs_down[i, :12, :] = jnp.where(lane < 64, r0[x, 0, own, :], pltpu.roll(density[0], 64, 1))
        return c

    columns(0, 12, 4, prepare, 0)
    pl.semaphore_wait(barrier, len(met))

    along_z = [
        sender.start(zs_up.at[:, :12, :], zr_below.at[:, :12, :], (0, 0, 1)),
        sender.start(zs_down.at[:, :12, :], zr_above.at[:, :12, :], (0, 0, -1)),
    ]
    fine_rho = sender.exchange(rho0, l0, 5, AROUND, (0, 4))

    wait_recv(along_z)
    gz = lax.axis_index("gz")
    inside = jnp.where(lane < 64, jnp.where(gz == sizes["gz"] - 1, 0.0, 1.0), jnp.where(gz == 0, 0.0, 1.0))

    def ends(i, c):
        below, above = zr_below[i, :12, :], zr_above[i, :12, :]
        r0[i + l0["h"], 4, own, :] = jnp.where(lane < 64, above, below)
        rho0[i + l0["h"], 4, own, :] = inside * pltpu.roll(jnp.where(lane < 64, below, above), 64, 1)
        return c

    columns(0, 12, 6, ends, 0)
    fine_rho += sender.exchange(rho0, l0, 5, AROUND, (4, 5))
    fine_r = sender.exchange(r0, l0, 4, AROUND)

    restricted(rho0, rho1, l0, l1)
    restricted(rho1, rho2, l1, l2)
    density1 = sender.exchange(rho1, l1, 7, diamond(6, 7, 2))
    density2 = sender.exchange(rho2, l2, 8, line_y2)

    wait_recv(fine_rho)
    wait_send(fine_rho)
    clear_outside(rho0, l0, 5, sizes)
    coefficients(rho0, co0, l0, 4, 2.0, 1)
    wait_recv(fine_r)
    wait_send(fine_r)
    begin(r0, co0[4], d01, l0, 4, first, 4)
    smooth(d01, r0, d02, co0, l0, 3, *pairs[0], 3)
    smooth(d02, r0, d03, co0, l0, 2, *pairs[1], 4)
    smooth(d03, r0, d04, co0, l0, 1, *pairs[2], 4)

    def finish_down0(i, ys, here, applied):
        up0[i, :, ys, :] = r0[i, :, ys, :] - applied
        x0[i, :, ys, :] = (d01[i, :, ys, :] + d02[i, :, ys, :]) + (d03[i, :, ys, :] + here)

    sweep(d04, co0, l0, 0, 4, finish_down0)

    restricted(up0, r1, l0, l1)
    second = sender.exchange(r1, l1, 4, AROUND)
    wait_recv(density2)
    density2x = sender.exchange(rho2, l2, 8, line_x2, whole_y=True)
    back0 = sender.exchange(up0, l0, 4, AROUND)
    wait_recv(density1)
    wait_send(density1)
    clear_outside(rho1, l1, 7, sizes)
    coefficients(rho1, co1, l1, 6, 0.5, 2)
    wait_recv(second)
    wait_send(second)
    begin(r1, co1[4], d11, l1, 4, first, 7)
    smooth(d11, r1, d12, co1, l1, 3, *pairs[0], 6)
    smooth(d12, r1, d13, co1, l1, 2, *pairs[1], 5)
    smooth(d13, r1, d14, co1, l1, 1, *pairs[2], 8)

    def finish_down1(i, ys, here, applied):
        up1[i, :, ys, :] = r1[i, :, ys, :] - applied
        x1[i, :, ys, :] = (d11[i, :, ys, :] + d12[i, :, ys, :]) + (d13[i, :, ys, :] + here)

    sweep(d14, co1, l1, 0, 6, finish_down1)

    restricted(up1, r2, l1, l2)
    third = sender.exchange(r2, l2, 7, coarse_offsets)
    back1 = sender.exchange(up1, l1, 6, AROUND) + sender.exchange(x1, l1, 3, AROUND)
    wait_recv(density2x)
    wait_send(density2 + density2x)
    clear_outside(rho2, l2, 8, sizes)
    coefficients(rho2, co2, l2, 7, 0.125, 2)
    wait_recv(third)
    wait_send(third)
    begin(r2, co2[4], d21, l2, 7, first2, 17)

    def copy_total(i, c):
        x2[i, :, l2["h"] : l2["h"] + 3, :] = d21[i, :, l2["h"] : l2["h"] + 3, :]
        return c

    columns(l2["h"], l2["h"] + 3, 3, copy_total, 0)
    v, d = d21, d22
    for k, (alpha, beta) in enumerate(pairs2):
        smooth(v, r2, d, co2, l2, 6 - k, alpha, beta, 8)
        v, d = d, v

        def add_total(i, c, v=v):
            x2[i, :, l2["h"] : l2["h"] + 3, :] = x2[i, :, l2["h"] : l2["h"] + 3, :] + v[i, :, l2["h"] : l2["h"] + 3, :]
            return c

        columns(l2["h"], l2["h"] + 3, 3, add_total, 0)

    fourth = sender.exchange(x2, l2, 4, diamond(3, 4, 2))
    wait_recv(back1)
    wait_send(back1)
    wait_recv(fourth)
    clear_outside(x2, l2, 4, sizes)
    prolonged(x2, u1, l2, l1, 4)
    smooth(u1, up1, d11, co1, l1, 6, None, first, 6)
    smooth(d11, up1, d12, co1, l1, 5, *pairs[0], 8)
    smooth(d12, up1, d13, co1, l1, 4, *pairs[1], 7)
    smooth(d13, up1, d14, co1, l1, 3, *pairs[2], 6)
    reach1 = pl.ds(l1["h"] - 3, 12)

    def finish_up1(i, c):
        total = (x1[i, :, reach1, :] + u1[i, :, reach1, :]) + (d11[i, :, reach1, :] + d12[i, :, reach1, :])
        x1[i, :, reach1, :] = total + (d13[i, :, reach1, :] + d14[i, :, reach1, :])
        return c

    columns(l1["h"] - 3, l1["h"] + 9, 6, finish_up1, 0)
    clear_outside(x1, l1, 3, sizes)

    prolonged(x1, u0, l1, l0, 3)
    wait_recv(back0)
    wait_send(back0)
    smooth(u0, up0, d01, co0, l0, 4, None, first, 3)
    smooth(d01, up0, d02, co0, l0, 3, *pairs[0], 3)
    smooth(d02, up0, d03, co0, l0, 2, *pairs[1], 4)
    smooth(d03, up0, d04, co0, l0, 1, *pairs[2], 4)

    def finish_up0(i, ys, here, applied):
        j = i - l0["h"]
        total = (x0[i, :, ys, :] + u0[i, :, ys, :]) + (d01[i, :, ys, :] + d02[i, :, ys, :])
        total = total + (d03[i, :, ys, :] + here)
        rest = up0[i, :, ys, :] - applied
        for t in range(4):
            out_x[j, :, 128 * t : 128 * t + 128] = total[t]
            out_r[j, :, 128 * t : 128 * t + 128] = rest[t]

    sweep(d04, co0, l0, 0, 4, finish_up0)
    wait_send(along_z)
    wait_send(fourth)


COPIES = 2 + 24 + 12 + 12 + 8 + 6 + 8 + 24 + 16 + 12


def per_device(sizes, right_side, phase):
    def field(level):
        return pltpu.VMEM((level["cols"], level["t"], level["rows"], 128), jnp.float32)

    l0, l1, l2 = LEVELS
    shape = right_side.shape
    result = pltpu.VMEM(shape, jnp.float32)
    whole = pl.BlockSpec(memory_space=pltpu.VMEM)
    return pl.pallas_call(
        functools.partial(kernel, sizes),
        out_shape=(result, result),
        in_specs=[pl.BlockSpec(memory_space=pl.ANY)] * 2,
        out_specs=(whole, whole),
        scratch_shapes=[field(l0)] * 14
        + [field(l1)] * 14
        + [field(l2)] * 10
        + [pltpu.VMEM(shape, jnp.int32)]
        + [pltpu.VMEM((12, 16, 128), jnp.float32)] * 4
        + [pltpu.SemaphoreType.DMA((5,))]
        + [pltpu.SemaphoreType.DMA((COPIES,))] * 2,
        compiler_params=pltpu.CompilerParams(
            collective_id=0, has_side_effects=True, vmem_limit_bytes=56 * 1024 * 1024
        ),
        cost_estimate=pl.CostEstimate(flops=60_000_000, bytes_accessed=1_200_000, transcendentals=0),
        name="cycle",
    )(right_side, phase)


def solution(mesh):
    spec = P("gx", "gy", "gz")
    return jax.shard_map(
        functools.partial(per_device, dict(mesh.shape)),
        mesh=mesh,
        in_specs=(spec, spec),
        out_specs=(spec, spec),
        check_vma=False,
    )
```

```python
import functools

import jax
import jax.numpy as jnp
from jax import lax
from jax.experimental import pallas as pl
from jax.experimental.pallas import tpu as pltpu
from jax.sharding import PartitionSpec as P

MESH = pl.DeviceIdType.MESH
DEGREE = 4
COARSE_ITERS = 8
HEAVY = 20.0
SMOOTH_LOWEST = 0.3
COARSE_LOWEST = 0.02
UPPER = 2.0

LEVELS = (
    dict(n=12, h=6, t=5, cols=24, rows=32),
    dict(n=6, h=8, t=3, cols=22, rows=32),
    dict(n=3, h=8, t=2, cols=19, rows=32),
)


def weights(lowest, degree):
    middle, radius = (UPPER + lowest) / 2.0, (UPPER - lowest) / 2.0
    sharpness = middle / radius
    old = 1.0 / sharpness
    pairs = []
    for _ in range(1, degree):
        new = 1.0 / (2.0 * sharpness - old)
        pairs.append((new * old, 2.0 * new / radius))
        old = new
    return 1.0 / middle, pairs


def columns(lo, hi, unroll, body, carry):
    trips = (hi - lo) // unroll

    def several(k, c):
        for j in range(unroll):
            c = body(lo + k * unroll + j, c)
        return c

    if trips > 1:
        carry = lax.fori_loop(0, trips, several, carry)
    elif trips == 1:
        carry = several(0, carry)
    for i in range(lo + trips * unroll, hi):
        carry = body(i, carry)
    return carry


def lanes(shape):
    return lax.broadcasted_iota(jnp.int32, shape, len(shape) - 1)


def shifted(blocks, towards):
    count = len(blocks)
    shape = blocks[0].shape
    edge = lanes(shape) == (127 if towards > 0 else 0)
    rolled = [pltpu.roll(v, 127 if towards > 0 else 1, 1) for v in blocks]
    return [jnp.where(edge, rolled[(t + towards) % count], rolled[t]) for t in range(count)]


def split(block):
    return [block[t] for t in range(block.shape[0])]


def picked(value, index):
    return jnp.take_along_axis(value, index, axis=1)


def halved(blocks):
    lane = lanes(blocks[0].shape)
    index = (2 * lane) % 128
    pairs = [picked(v + pltpu.roll(v, 127, 1), index) for v in blocks]
    out = [jnp.where(lane < 64, pairs[2 * t], pairs[2 * t + 1]) for t in range(len(blocks) // 2)]
    out.append(pairs[-1])
    return out


def doubled(blocks):
    lane = lanes(blocks[0].shape)
    low, high = lane // 2, 64 + lane // 2
    out = []
    for v in blocks[:-1]:
        out += [picked(v, low), picked(v, high)]
    out.append(picked(blocks[-1], jnp.where(lane < 64, low, high)))
    return out


def near(o, n):
    return (abs(o) - 1) * n + 1 if o else 0


def reach(offset, n, w):
    return max(offset * n, -w), min(offset * n + n, n + w)


class Group:
    def __init__(self, send_sem, recv_sem, blank):
        self.send, self.recv, self.blank, self.count = send_sem, recv_sem, blank, 0

    def wait(self, sem):
        rows = self.blank.at[0 : self.count, :]
        pltpu.make_async_copy(rows, rows, sem).wait()

    def wait_recv(self):
        self.wait(self.recv)

    def wait_send(self):
        self.wait(self.send)


class Sender:
    def __init__(self, send_sems, recv_sems, blank, sizes):
        self.send, self.recv, self.blank, self.sizes = send_sems, recv_sems, blank, sizes
        self.groups = []

    def target(self, offset):
        place = []
        for axis, o in zip(("gx", "gy", "gz"), offset):
            size = self.sizes[axis]
            place.append(lax.rem(lax.axis_index(axis) + (o + 4 * size), size) if o else lax.axis_index(axis))
        return tuple(place)

    def group(self):
        k = len(self.groups)
        self.groups.append(Group(self.send.at[k], self.recv.at[k], self.blank))
        return self.groups[-1]

    def start(self, group, src, dst, offset):
        copy = pltpu.make_async_remote_copy(
            src_ref=src,
            dst_ref=dst,
            send_sem=group.send,
            recv_sem=group.recv,
            device_id=self.target(offset),
            device_id_type=MESH,
        )
        copy.start()
        rows = 1
        for size in src.shape[:-1]:
            rows *= size
        group.count += rows

    def exchange(self, group, ref, level, w, offsets, tiles=None, whole_y=False):
        n, h = level["n"], level["h"]
        t0, t1 = tiles or (0, level["t"])
        for ox, oy in offsets:
            x0, x1 = reach(ox, n, w - near(oy, n))
            y0, y1 = (-w, n + w) if whole_y else reach(oy, n, w - near(ox, n))
            sx, sy = x0 - ox * n + h, y0 - oy * n + h
            self.start(
                group,
                ref.at[sx : sx + x1 - x0, t0:t1, sy : sy + y1 - y0, :],
                ref.at[x0 + h : x1 + h, t0:t1, y0 + h : y1 + h, :],
                (-ox, -oy, 0),
            )
        return group


def diamond(n, w, most):
    found = []
    for ox in range(-most, most + 1):
        for oy in range(-most, most + 1):
            if (ox or oy) and near(ox, n) + near(oy, n) <= w:
                found.append((ox, oy))
    return sorted(found, key=lambda o: -abs(o[0]) - abs(o[1]))


AROUND = diamond(1, 2, 1)


def clear_outside(ref, level, w, sizes):
    n, h, t = level["n"], level["h"], level["t"]

    def clear(x0, x1, y0, y1):
        zero = jnp.zeros((t, y1 - y0, 128), jnp.float32)

        def body(i, c):
            ref[i, :, y0:y1, :] = zero
            return c

        lax.fori_loop(x0, x1, body, 0)

    gx, gy = lax.axis_index("gx"), lax.axis_index("gy")
    for k in range(-(-w // n)):
        below, above = (h - w, h - k * n), (h + n + k * n, h + n + w)
        every = (h - w, h + n + w)
        pl.when(gx == k)(functools.partial(clear, *below, *every))
        pl.when(gx == sizes["gx"] - 1 - k)(functools.partial(clear, *above, *every))
        pl.when(gy == k)(functools.partial(clear, *every, *below))
        pl.when(gy == sizes["gy"] - 1 - k)(functools.partial(clear, *every, *above))


def inverse_of(value):
    guess = pl.reciprocal(value, approx=True)
    return guess * (2.0 - value * guess)


def conduct(a, b, scale):
    return scale * inverse_of(jnp.maximum(a + b, 0.5))


def coefficients(rho, co, level, w, scale, unroll):
    bx, by, bzp, bzm, iv = co
    n, h = level["n"], level["h"]
    lo, hi, rows = h - w, h + n + w, n + 2 * w
    ys = pl.ds(lo, rows)

    def body(i, before):
        here = rho[i, :, ys, :]
        after = conduct(here, rho[i + 1, :, ys, :], scale)
        bx[i, :, ys, :] = after
        by[i, :, pl.ds(lo - 1, rows + 1), :] = conduct(
            rho[i, :, pl.ds(lo - 1, rows + 1), :], rho[i, :, pl.ds(lo, rows + 1), :], scale
        )
        above = jnp.stack([conduct(a, b, scale) for a, b in zip(split(here), shifted(split(here), 1))])
        below = jnp.stack(shifted(split(above), -1))
        bzp[i, :, ys, :] = above
        bzm[i, :, ys, :] = below
        total = (before + after) + (above + below) + (by[i, :, ys, :] + by[i, :, pl.ds(lo - 1, rows), :])
        inverse = jnp.where(here > 0.0, inverse_of(total), 0.0)
        iv[i, :, ys, :] = inverse
        return after

    start = conduct(rho[lo - 1, :, ys, :], rho[lo, :, ys, :], scale)
    bx[lo - 1, :, ys, :] = start
    columns(lo, hi, unroll, body, start)


def begin(r, iv, d, level, w, weight, unroll):
    n, h = level["n"], level["h"]
    ys = pl.ds(h - w, n + 2 * w)

    def body(i, c):
        d[i, :, ys, :] = weight * (iv[i, :, ys, :] * r[i, :, ys, :])
        return c

    columns(h - w, h + n + w, unroll, body, 0)


def sweep(v, co, level, w, unroll, finish, tiles=None):
    bx, by, bzp, bzm, _ = co
    n, h, t = level["n"], level["h"], level["t"]
    lo, hi, rows = h - w, h + n + w, n + 2 * w
    ys, up, down = pl.ds(lo, rows), pl.ds(lo + 1, rows), pl.ds(lo - 1, rows)

    def body(i, carry):
        here, before = carry
        after = v[i + 1, :, ys, :]
        flux = bx[i, :, ys, :] * (here - after)
        parts = split(here)
        zp = jnp.stack(shifted(parts, 1))
        zm = jnp.stack(shifted(parts, -1))
        total = (flux - before) + bzp[i, :, ys, :] * (here - zp) + bzm[i, :, ys, :] * (here - zm)
        total = total + by[i, :, ys, :] * (here - v[i, :, up, :])
        total = total + by[i, :, down, :] * (here - v[i, :, down, :])
        finish(i, ys, here, total)
        return after, flux

    here = v[lo, :, ys, :]
    before = bx[lo - 1, :, ys, :] * (v[lo - 1, :, ys, :] - here)
    columns(lo, hi, unroll, body, (here, before))


def smooth(v, r, d, co, level, w, alpha, beta, unroll, total=None):
    iv = co[4]

    def finish(i, ys, here, applied):
        rest = r[i, :, ys, :] - applied
        r[i, :, ys, :] = rest
        new = beta * (iv[i, :, ys, :] * rest)
        if alpha is not None:
            new = alpha * here + new
        d[i, :, ys, :] = new
        if total is not None:
            total[i, :, ys, :] = total[i, :, ys, :] + new

    sweep(v, co, level, w, unroll, finish)


def restricted(fine, coarse, level_fine, level_coarse):
    h, n, hc = level_fine["h"], level_coarse["n"], level_coarse["h"]

    def body(i, c):
        x = h + 2 * i
        even, odd = pl.ds(h, n, stride=2), pl.ds(h + 1, n, stride=2)
        blocks = []
        for t in range(level_fine["t"]):
            both = fine[x, t, even, :] + fine[x, t, odd, :]
            both = both + (fine[x + 1, t, even, :] + fine[x + 1, t, odd, :])
            blocks.append(both)
        coarse[hc + i, :, hc : hc + n, :] = jnp.stack(halved(blocks)) * 0.125
        return c

    for i in range(n):
        body(i, 0)


def prolonged(coarse, fine, level_coarse, level_fine, w):
    hc, h, n = level_coarse["h"], level_fine["h"], level_coarse["n"]
    count = n + 2 * w

    def body(k, c):
        block = doubled(split(coarse[hc - w + k, :, hc - w : hc - w + count, :]))
        for t, v in enumerate(block):
            for x in (0, 1):
                for y in (0, 1):
                    fine[h - 2 * w + 2 * k + x, t, pl.ds(h - 2 * w + y, count, stride=2), :] = v
        return c

    columns(0, count, 3, body, 0)


def kernel(sizes, rhs, phase, out_x, out_r, *scratch):
    scratch = list(scratch)

    def take(count):
        taken, scratch[:count] = scratch[:count], []
        return taken

    rho0, r0, up0, u0, x0, d01, d02, d03, d04 = take(9)
    co0 = take(5)
    rho1, r1, up1, u1, x1, d11, d12, d13, d14 = take(9)
    co1 = take(5)
    rho2, r2, x2, d21, d22 = take(5)
    co2 = take(5)
    kind, zs_up, zs_down, zr_below, zr_above, blank, local_sems, send_sems, recv_sems = take(9)
    l0, l1, l2 = LEVELS
    sender = Sender(send_sems, recv_sems, blank, sizes)
    first, pairs = weights(SMOOTH_LOWEST, DEGREE)
    first2, pairs2 = weights(COARSE_LOWEST, COARSE_ITERS)
    own = slice(l0["h"], l0["h"] + 12)

    loads = [pltpu.make_async_copy(phase, kind, local_sems.at[4])]
    for t in range(4):
        loads.append(
            pltpu.make_async_copy(rhs.at[:, :, 128 * t : 128 * t + 128], r0.at[own, t, own, :], local_sems.at[t])
        )
    for copy in loads:
        copy.start()

    coarse_offsets = diamond(3, 7, 3)
    line_y2 = [(0, o) for o in (3, -3, 2, -2, 1, -1)]
    line_x2 = [(o, 0) for _, o in line_y2]
    met = {(ox, oy, 0) for ox, oy in coarse_offsets + line_y2 + line_x2 + AROUND} | {(0, 0, 1), (0, 0, -1)}
    barrier = pltpu.get_barrier_semaphore()
    for offset in sorted(met):
        pl.semaphore_signal(barrier, inc=1, device_id=sender.target(offset), device_id_type=MESH)

    lane = lanes((12, 128))
    for copy in loads:
        copy.wait()

    def prepare(i, c):
        x = i + l0["h"]
        density = []
        for t in range(4):
            part = slice(128 * t, 128 * t + 128)
            density.append(jnp.where(kind[i, :, part] == 1, HEAVY, 1.0).astype(jnp.float32))
            rho0[x, t, own, :] = density[t]
        zs_up[i, :12, :] = jnp.where(lane >= 64, r0[x, 3, own, :], pltpu.roll(density[3], 64, 1))
        zs_down[i, :12, :] = jnp.where(lane < 64, r0[x, 0, own, :], pltpu.roll(density[0], 64, 1))
        return c

    columns(0, 12, 4, prepare, 0)
    pl.semaphore_wait(barrier, len(met))

    along_z = sender.group()
    sender.start(along_z, zs_up.at[:, :12, :], zr_below.at[:, :12, :], (0, 0, 1))
    sender.start(along_z, zs_down.at[:, :12, :], zr_above.at[:, :12, :], (0, 0, -1))
    fine_rho = sender.exchange(sender.group(), rho0, l0, 5, AROUND, (0, 4))

    along_z.wait_recv()
    gz = lax.axis_index("gz")
    inside = jnp.where(lane < 64, jnp.where(gz == sizes["gz"] - 1, 0.0, 1.0), jnp.where(gz == 0, 0.0, 1.0))

    def ends(i, c):
        below, above = zr_below[i, :12, :], zr_above[i, :12, :]
        r0[i + l0["h"], 4, own, :] = jnp.where(lane < 64, above, below)
        rho0[i + l0["h"], 4, own, :] = inside * pltpu.roll(jnp.where(lane < 64, below, above), 64, 1)
        return c

    columns(0, 12, 6, ends, 0)
    fine_rho4 = sender.exchange(sender.group(), rho0, l0, 5, AROUND, (4, 5))
    fine_r = sender.exchange(sender.group(), r0, l0, 4, AROUND)

    restricted(rho0, rho1, l0, l1)
    restricted(rho1, rho2, l1, l2)
    density1 = sender.exchange(sender.group(), rho1, l1, 7, diamond(6, 7, 2))
    density2 = sender.exchange(sender.group(), rho2, l2, 8, line_y2)

    fine_rho.wait_recv()
    fine_rho4.wait_recv()
    clear_outside(rho0, l0, 5, sizes)
    coefficients(rho0, co0, l0, 4, 2.0, 2)
    fine_r.wait_recv()
    fine_r.wait_send()
    begin(r0, co0[4], d01, l0, 4, first, 4)
    smooth(d01, r0, d02, co0, l0, 3, *pairs[0], 9)
    smooth(d02, r0, d03, co0, l0, 2, *pairs[1], 8)
    smooth(d03, r0, d04, co0, l0, 1, *pairs[2], 7)

    def finish_down0(i, ys, here, applied):
        up0[i, :, ys, :] = r0[i, :, ys, :] - applied
        x0[i, :, ys, :] = (d01[i, :, ys, :] + d02[i, :, ys, :]) + (d03[i, :, ys, :] + here)

    sweep(d04, co0, l0, 0, 6, finish_down0)

    restricted(up0, r1, l0, l1)
    second = sender.exchange(sender.group(), r1, l1, 4, AROUND)
    density2.wait_recv()
    density2x = sender.exchange(sender.group(), rho2, l2, 8, line_x2, whole_y=True)
    back0 = sender.exchange(sender.group(), up0, l0, 4, AROUND)
    density1.wait_recv()
    density1.wait_send()
    clear_outside(rho1, l1, 7, sizes)
    coefficients(rho1, co1, l1, 6, 0.5, 2)
    second.wait_recv()
    second.wait_send()
    begin(r1, co1[4], d11, l1, 4, first, 7)
    smooth(d11, r1, d12, co1, l1, 3, *pairs[0], 12)
    smooth(d12, r1, d13, co1, l1, 2, *pairs[1], 10)
    smooth(d13, r1, d14, co1, l1, 1, *pairs[2], 8)

    def finish_down1(i, ys, here, applied):
        up1[i, :, ys, :] = r1[i, :, ys, :] - applied
        x1[i, :, ys, :] = (d11[i, :, ys, :] + d12[i, :, ys, :]) + (d13[i, :, ys, :] + here)

    sweep(d14, co1, l1, 0, 6, finish_down1)

    restricted(up1, r2, l1, l2)
    third = sender.exchange(sender.group(), r2, l2, 7, coarse_offsets)
    back1 = sender.exchange(sender.group(), up1, l1, 6, AROUND)
    sender.exchange(back1, x1, l1, 3, AROUND)
    density2x.wait_recv()
    density2.wait_send()
    density2x.wait_send()
    clear_outside(rho2, l2, 8, sizes)
    coefficients(rho2, co2, l2, 7, 0.125, 2)
    third.wait_recv()
    third.wait_send()
    begin(r2, co2[4], d21, l2, 7, first2, 17)

    def copy_total(i, c):
        x2[i, :, l2["h"] : l2["h"] + 3, :] = d21[i, :, l2["h"] : l2["h"] + 3, :]
        return c

    columns(l2["h"], l2["h"] + 3, 3, copy_total, 0)
    v, d = d21, d22
    for k, (alpha, beta) in enumerate(pairs2):
        smooth(v, r2, d, co2, l2, 6 - k, alpha, beta, 15)
        v, d = d, v

        def add_total(i, c, v=v):
            x2[i, :, l2["h"] : l2["h"] + 3, :] = x2[i, :, l2["h"] : l2["h"] + 3, :] + v[i, :, l2["h"] : l2["h"] + 3, :]
            return c

        columns(l2["h"], l2["h"] + 3, 3, add_total, 0)

    fourth = sender.exchange(sender.group(), x2, l2, 4, diamond(3, 4, 2))
    back1.wait_recv()
    back1.wait_send()
    fourth.wait_recv()
    clear_outside(x2, l2, 4, sizes)
    prolonged(x2, u1, l2, l1, 4)
    smooth(u1, up1, d11, co1, l1, 6, None, first, 9)
    smooth(d11, up1, d12, co1, l1, 5, *pairs[0], 8)
    smooth(d12, up1, d13, co1, l1, 4, *pairs[1], 14)
    smooth(d13, up1, d14, co1, l1, 3, *pairs[2], 12)
    reach1 = pl.ds(l1["h"] - 3, 12)

    def finish_up1(i, c):
        total = (x1[i, :, reach1, :] + u1[i, :, reach1, :]) + (d11[i, :, reach1, :] + d12[i, :, reach1, :])
        x1[i, :, reach1, :] = total + (d13[i, :, reach1, :] + d14[i, :, reach1, :])
        return c

    columns(l1["h"] - 3, l1["h"] + 9, 6, finish_up1, 0)
    clear_outside(x1, l1, 3, sizes)

    prolonged(x1, u0, l1, l0, 3)
    back0.wait_recv()
    back0.wait_send()
    smooth(u0, up0, d01, co0, l0, 4, None, first, 10)
    smooth(d01, up0, d02, co0, l0, 3, *pairs[0], 9)
    smooth(d02, up0, d03, co0, l0, 2, *pairs[1], 8)
    smooth(d03, up0, d04, co0, l0, 1, *pairs[2], 7)

    def finish_up0(i, ys, here, applied):
        j = i - l0["h"]
        total = (x0[i, :, ys, :] + u0[i, :, ys, :]) + (d01[i, :, ys, :] + d02[i, :, ys, :])
        total = total + (d03[i, :, ys, :] + here)
        rest = up0[i, :, ys, :] - applied
        for t in range(4):
            out_x[j, :, 128 * t : 128 * t + 128] = total[t]
            out_r[j, :, 128 * t : 128 * t + 128] = rest[t]

    sweep(d04, co0, l0, 0, 6, finish_up0)
    along_z.wait_send()
    fine_rho.wait_send()
    fine_rho4.wait_send()
    fourth.wait_send()


GROUPS = 12


def per_device(sizes, right_side, phase):
    def field(level):
        return pltpu.VMEM((level["cols"], level["t"], level["rows"], 128), jnp.float32)

    l0, l1, l2 = LEVELS
    shape = right_side.shape
    result = pltpu.VMEM(shape, jnp.float32)
    whole = pl.BlockSpec(memory_space=pltpu.VMEM)
    return pl.pallas_call(
        functools.partial(kernel, sizes),
        out_shape=(result, result),
        in_specs=[pl.BlockSpec(memory_space=pl.ANY)] * 2,
        out_specs=(whole, whole),
        scratch_shapes=[field(l0)] * 14
        + [field(l1)] * 14
        + [field(l2)] * 10
        + [pltpu.VMEM(shape, jnp.int32)]
        + [pltpu.VMEM((12, 16, 128), jnp.float32)] * 4
        + [pltpu.VMEM((1280, 128), jnp.float32)]
        + [pltpu.SemaphoreType.DMA((5,))]
        + [pltpu.SemaphoreType.DMA((GROUPS,))] * 2,
        compiler_params=pltpu.CompilerParams(
            collective_id=0, has_side_effects=True, vmem_limit_bytes=56 * 1024 * 1024
        ),
        cost_estimate=pl.CostEstimate(flops=60_000_000, bytes_accessed=1_200_000, transcendentals=0),
        name="cycle",
    )(right_side, phase)


def solution(mesh):
    spec = P("gx", "gy", "gz")
    return jax.shard_map(
        functools.partial(per_device, dict(mesh.shape)),
        mesh=mesh,
        in_specs=(spec, spec),
        out_specs=(spec, spec),
        check_vma=False,
    )
```

```python
import functools

import jax
import jax.numpy as jnp
from jax import lax
from jax.experimental import pallas as pl
from jax.experimental.pallas import tpu as pltpu
from jax.sharding import PartitionSpec as P

MESH = pl.DeviceIdType.MESH
DEGREE = 4
COARSE_ITERS = 8
HEAVY = 20.0
SMOOTH_LOWEST = 0.3
COARSE_LOWEST = 0.02
UPPER = 2.0

LEVELS = (
    dict(n=12, h=6, t=5, cols=24, rows=32),
    dict(n=6, h=8, t=3, cols=22, rows=32),
    dict(n=3, h=8, t=2, cols=19, rows=32),
)


def weights(lowest, degree):
    middle, radius = (UPPER + lowest) / 2.0, (UPPER - lowest) / 2.0
    sharpness = middle / radius
    old = 1.0 / sharpness
    pairs = []
    for _ in range(1, degree):
        new = 1.0 / (2.0 * sharpness - old)
        pairs.append((new * old, 2.0 * new / radius))
        old = new
    return 1.0 / middle, pairs


def columns(lo, hi, unroll, body, carry):
    trips = (hi - lo) // unroll

    def several(k, c):
        for j in range(unroll):
            c = body(lo + k * unroll + j, c)
        return c

    if trips > 1:
        carry = lax.fori_loop(0, trips, several, carry)
    elif trips == 1:
        carry = several(0, carry)
    for i in range(lo + trips * unroll, hi):
        carry = body(i, carry)
    return carry


def lanes(shape):
    return lax.broadcasted_iota(jnp.int32, shape, len(shape) - 1)


def shifted(blocks, towards):
    count = len(blocks)
    shape = blocks[0].shape
    edge = lanes(shape) == (127 if towards > 0 else 0)
    rolled = [pltpu.roll(v, 127 if towards > 0 else 1, 1) for v in blocks]
    return [jnp.where(edge, rolled[(t + towards) % count], rolled[t]) for t in range(count)]


def split(block):
    return [block[t] for t in range(block.shape[0])]


def picked(value, index):
    return jnp.take_along_axis(value, index, axis=1)


def halved(blocks):
    lane = lanes(blocks[0].shape)
    index = (2 * lane) % 128
    pairs = [picked(v + pltpu.roll(v, 127, 1), index) for v in blocks]
    out = [jnp.where(lane < 64, pairs[2 * t], pairs[2 * t + 1]) for t in range(len(blocks) // 2)]
    out.append(pairs[-1])
    return out


def doubled(blocks):
    lane = lanes(blocks[0].shape)
    low, high = lane // 2, 64 + lane // 2
    out = []
    for v in blocks[:-1]:
        out += [picked(v, low), picked(v, high)]
    out.append(picked(blocks[-1], jnp.where(lane < 64, low, high)))
    return out


def near(o, n):
    return (abs(o) - 1) * n + 1 if o else 0


def reach(offset, n, w):
    return max(offset * n, -w), min(offset * n + n, n + w)


class Group:
    def __init__(self, send_sem, recv_sem, blank):
        self.send, self.recv, self.blank, self.count = send_sem, recv_sem, blank, 0

    def wait(self, sem):
        rows = self.blank.at[0 : self.count, :]
        pltpu.make_async_copy(rows, rows, sem).wait()

    def wait_recv(self):
        self.wait(self.recv)

    def wait_send(self):
        self.wait(self.send)


class Sender:
    def __init__(self, send_sems, recv_sems, blank, sizes):
        self.send, self.recv, self.blank, self.sizes = send_sems, recv_sems, blank, sizes
        self.groups = []

    def target(self, offset):
        place = []
        for axis, o in zip(("gx", "gy", "gz"), offset):
            size = self.sizes[axis]
            place.append(lax.rem(lax.axis_index(axis) + (o + 4 * size), size) if o else lax.axis_index(axis))
        return tuple(place)

    def group(self):
        k = len(self.groups)
        self.groups.append(Group(self.send.at[k], self.recv.at[k], self.blank))
        return self.groups[-1]

    def start(self, group, src, dst, offset):
        copy = pltpu.make_async_remote_copy(
            src_ref=src,
            dst_ref=dst,
            send_sem=group.send,
            recv_sem=group.recv,
            device_id=self.target(offset),
            device_id_type=MESH,
        )
        copy.start()
        rows = 1
        for size in src.shape[:-1]:
            rows *= size
        group.count += rows

    def exchange(self, group, ref, level, w, offsets, tiles=None, whole_y=False):
        n, h = level["n"], level["h"]
        t0, t1 = tiles or (0, level["t"])
        for ox, oy in offsets:
            x0, x1 = reach(ox, n, w - near(oy, n))
            y0, y1 = (-w, n + w) if whole_y else reach(oy, n, w - near(ox, n))
            sx, sy = x0 - ox * n + h, y0 - oy * n + h
            self.start(
                group,
                ref.at[sx : sx + x1 - x0, t0:t1, sy : sy + y1 - y0, :],
                ref.at[x0 + h : x1 + h, t0:t1, y0 + h : y1 + h, :],
                (-ox, -oy, 0),
            )
        return group


def diamond(n, w, most):
    found = []
    for ox in range(-most, most + 1):
        for oy in range(-most, most + 1):
            if (ox or oy) and near(ox, n) + near(oy, n) <= w:
                found.append((ox, oy))
    return sorted(found, key=lambda o: -abs(o[0]) - abs(o[1]))


AROUND = diamond(1, 2, 1)
FACES = [o for o in AROUND if 0 in o]
CORNERS = [o for o in AROUND if 0 not in o]


def clear_outside(ref, level, w, sizes, tiles=None):
    n, h = level["n"], level["h"]
    t0, t1 = tiles or (0, level["t"])

    def clear(x0, x1, y0, y1):
        zero = jnp.zeros((t1 - t0, y1 - y0, 128), jnp.float32)

        def body(i, c):
            ref[i, t0:t1, y0:y1, :] = zero
            return c

        lax.fori_loop(x0, x1, body, 0)

    gx, gy = lax.axis_index("gx"), lax.axis_index("gy")
    for k in range(-(-w // n)):
        below, above = (h - w, h - k * n), (h + n + k * n, h + n + w)
        every = (h - w, h + n + w)
        pl.when(gx == k)(functools.partial(clear, *below, *every))
        pl.when(gx == sizes["gx"] - 1 - k)(functools.partial(clear, *above, *every))
        pl.when(gy == k)(functools.partial(clear, *every, *below))
        pl.when(gy == sizes["gy"] - 1 - k)(functools.partial(clear, *every, *above))


def inverse_of(value):
    guess = pl.reciprocal(value, approx=True)
    return guess * (2.0 - value * guess)


def conduct(a, b, scale):
    return scale * inverse_of(jnp.maximum(a + b, 0.5))


def face_coefficients(rho, co, level, w, scale, unroll, tiles=None):
    bx, by = co[:2]
    n, h = level["n"], level["h"]
    lo, hi, rows = h - w, h + n + w, n + 2 * w
    ts, ys, ends = slice(*(tiles or (0, level["t"]))), pl.ds(lo, rows), pl.ds(lo - 1, rows + 1)

    def body(i, c):
        bx[i, ts, ys, :] = conduct(rho[i, ts, ys, :], rho[i + 1, ts, ys, :], scale)
        by[i, ts, ends, :] = conduct(rho[i, ts, ends, :], rho[i, ts, pl.ds(lo, rows + 1), :], scale)
        return c

    bx[lo - 1, ts, ys, :] = conduct(rho[lo - 1, ts, ys, :], rho[lo, ts, ys, :], scale)
    columns(lo, hi, unroll, body, 0)


def other_coefficients(rho, co, level, w, scale, unroll):
    bx, by, bzp, bzm, iv = co
    n, h = level["n"], level["h"]
    lo, hi, rows = h - w, h + n + w, n + 2 * w
    ys = pl.ds(lo, rows)

    def body(i, c):
        here = rho[i, :, ys, :]
        above = jnp.stack([conduct(a, b, scale) for a, b in zip(split(here), shifted(split(here), 1))])
        below = jnp.stack(shifted(split(above), -1))
        bzp[i, :, ys, :] = above
        bzm[i, :, ys, :] = below
        total = (bx[i - 1, :, ys, :] + bx[i, :, ys, :]) + (by[i, :, ys, :] + by[i, :, pl.ds(lo - 1, rows), :])
        iv[i, :, ys, :] = jnp.where(here > 0.0, inverse_of(total + (above + below)), 0.0)
        return c

    columns(lo, hi, unroll, body, 0)


def coefficients(rho, co, level, w, scale, unroll):
    face_coefficients(rho, co, level, w, scale, unroll)
    other_coefficients(rho, co, level, w, scale, unroll)


def begin(r, iv, d, level, w, weight, unroll):
    n, h = level["n"], level["h"]
    ys = pl.ds(h - w, n + 2 * w)

    def body(i, c):
        d[i, :, ys, :] = weight * (iv[i, :, ys, :] * r[i, :, ys, :])
        return c

    columns(h - w, h + n + w, unroll, body, 0)


def sweep(v, co, level, w, unroll, finish, tiles=None):
    bx, by, bzp, bzm, _ = co
    n, h, t = level["n"], level["h"], level["t"]
    lo, hi, rows = h - w, h + n + w, n + 2 * w
    ys, up, down = pl.ds(lo, rows), pl.ds(lo + 1, rows), pl.ds(lo - 1, rows)

    def body(i, carry):
        here, before = carry
        after = v[i + 1, :, ys, :]
        flux = bx[i, :, ys, :] * (here - after)
        parts = split(here)
        zp = jnp.stack(shifted(parts, 1))
        zm = jnp.stack(shifted(parts, -1))
        total = (flux - before) + bzp[i, :, ys, :] * (here - zp) + bzm[i, :, ys, :] * (here - zm)
        total = total + by[i, :, ys, :] * (here - v[i, :, up, :])
        total = total + by[i, :, down, :] * (here - v[i, :, down, :])
        finish(i, ys, here, total)
        return after, flux

    here = v[lo, :, ys, :]
    before = bx[lo - 1, :, ys, :] * (v[lo - 1, :, ys, :] - here)
    columns(lo, hi, unroll, body, (here, before))


def smooth(v, r, d, co, level, w, alpha, beta, unroll, total=None):
    iv = co[4]

    def finish(i, ys, here, applied):
        rest = r[i, :, ys, :] - applied
        r[i, :, ys, :] = rest
        new = beta * (iv[i, :, ys, :] * rest)
        if alpha is not None:
            new = alpha * here + new
        d[i, :, ys, :] = new
        if total is not None:
            total[i, :, ys, :] = total[i, :, ys, :] + new

    sweep(v, co, level, w, unroll, finish)


def restricted(fine, coarse, level_fine, level_coarse):
    h, n, hc = level_fine["h"], level_coarse["n"], level_coarse["h"]

    def body(i, c):
        x = h + 2 * i
        even, odd = pl.ds(h, n, stride=2), pl.ds(h + 1, n, stride=2)
        blocks = []
        for t in range(level_fine["t"]):
            both = fine[x, t, even, :] + fine[x, t, odd, :]
            both = both + (fine[x + 1, t, even, :] + fine[x + 1, t, odd, :])
            blocks.append(both)
        coarse[hc + i, :, hc : hc + n, :] = jnp.stack(halved(blocks)) * 0.125
        return c

    for i in range(n):
        body(i, 0)


def prolonged(coarse, fine, level_coarse, level_fine, w):
    hc, h, n = level_coarse["h"], level_fine["h"], level_coarse["n"]
    count = n + 2 * w

    def body(k, c):
        block = doubled(split(coarse[hc - w + k, :, hc - w : hc - w + count, :]))
        for t, v in enumerate(block):
            for x in (0, 1):
                for y in (0, 1):
                    fine[h - 2 * w + 2 * k + x, t, pl.ds(h - 2 * w + y, count, stride=2), :] = v
        return c

    columns(0, count, 6, body, 0)


def kernel(sizes, rhs, phase, out_x, out_r, *scratch):
    scratch = list(scratch)

    def take(count):
        taken, scratch[:count] = scratch[:count], []
        return taken

    rho0, r0, up0, u0, x0, d01, d02, d03, d04 = take(9)
    co0 = take(5)
    rho1, r1, up1, u1, x1, d11, d12, d13, d14 = take(9)
    co1 = take(5)
    rho2, r2, x2, d21, d22 = take(5)
    co2 = take(5)
    kind, zs_up, zs_down, zr_below, zr_above, blank, local_sems, send_sems, recv_sems = take(9)
    l0, l1, l2 = LEVELS
    sender = Sender(send_sems, recv_sems, blank, sizes)
    first, pairs = weights(SMOOTH_LOWEST, DEGREE)
    first2, pairs2 = weights(COARSE_LOWEST, COARSE_ITERS)
    own = slice(l0["h"], l0["h"] + 12)

    loads = [pltpu.make_async_copy(phase, kind, local_sems.at[4])]
    for t in range(4):
        loads.append(
            pltpu.make_async_copy(rhs.at[:, :, 128 * t : 128 * t + 128], r0.at[own, t, own, :], local_sems.at[t])
        )
    for copy in loads:
        copy.start()

    coarse_offsets = diamond(3, 7, 3)
    line_y2 = [(0, o) for o in (3, -3, 2, -2, 1, -1)]
    line_x2 = [(o, 0) for _, o in line_y2]
    met = sorted({(ox, oy, 0) for ox, oy in coarse_offsets + line_y2 + line_x2 + AROUND})
    gz = lax.axis_index("gz")
    has_below, has_above = gz > 0, gz < sizes["gz"] - 1
    barrier = pltpu.get_barrier_semaphore()

    def greet(offset):
        pl.semaphore_signal(barrier, inc=1, device_id=sender.target(offset), device_id_type=MESH)

    pl.when(has_above)(lambda: greet((0, 0, 1)))
    pl.when(has_below)(lambda: greet((0, 0, -1)))
    for offset in met:
        greet(offset)

    lane = lanes((12, 128))
    for copy in loads:
        copy.wait()

    def prepare(i, c):
        x = i + l0["h"]
        density = []
        for t in range(4):
            part = slice(128 * t, 128 * t + 128)
            density.append(jnp.where(kind[i, :, part] == 1, HEAVY, 1.0).astype(jnp.float32))
            rho0[x, t, own, :] = density[t]
        zs_up[i, :12, :] = jnp.where(lane >= 64, r0[x, 3, own, :], pltpu.roll(density[3], 64, 1))
        zs_down[i, :12, :] = jnp.where(lane < 64, r0[x, 0, own, :], pltpu.roll(density[0], 64, 1))
        return c

    columns(0, 12, 4, prepare, 0)
    beside = jnp.where(has_below, 1, 0) + jnp.where(has_above, 1, 0)
    pl.semaphore_wait(barrier, len(met) + beside)

    upwards, downwards = sender.group(), sender.group()

    @pl.when(has_above)
    def _():
        sender.start(upwards, zs_up.at[:, :12, :], zr_below.at[:, :12, :], (0, 0, 1))

    @pl.when(has_below)
    def _():
        sender.start(downwards, zs_down.at[:, :12, :], zr_above.at[:, :12, :], (0, 0, -1))

    @pl.when(jnp.logical_not(has_below))
    def _():
        zr_below[...] = jnp.zeros_like(zr_below)

    @pl.when(jnp.logical_not(has_above))
    def _():
        zr_above[...] = jnp.zeros_like(zr_above)

    fine_rho = sender.exchange(sender.group(), rho0, l0, 5, AROUND, (0, 4))
    fine_r = sender.exchange(sender.group(), r0, l0, 4, FACES, (0, 4))

    pl.when(has_below)(upwards.wait_recv)
    pl.when(has_above)(downwards.wait_recv)
    inside = jnp.where(lane < 64, jnp.where(has_above, 1.0, 0.0), jnp.where(has_below, 1.0, 0.0))

    def ends(i, c):
        below, above = zr_below[i, :12, :], zr_above[i, :12, :]
        r0[i + l0["h"], 4, own, :] = jnp.where(lane < 64, above, below)
        rho0[i + l0["h"], 4, own, :] = inside * pltpu.roll(jnp.where(lane < 64, below, above), 64, 1)
        return c

    columns(0, 12, 6, ends, 0)
    fine_rho4 = sender.exchange(sender.group(), rho0, l0, 5, AROUND, (4, 5))
    sender.exchange(fine_r, r0, l0, 4, CORNERS)
    sender.exchange(fine_r, r0, l0, 4, FACES, (4, 5))

    restricted(rho0, rho1, l0, l1)
    restricted(rho1, rho2, l1, l2)
    density1 = sender.exchange(sender.group(), rho1, l1, 7, diamond(6, 7, 2))
    density2 = sender.exchange(sender.group(), rho2, l2, 8, line_y2)

    fine_rho.wait_recv()
    clear_outside(rho0, l0, 5, sizes, (0, 4))
    face_coefficients(rho0, co0, l0, 4, 2.0, 2, (0, 4))
    fine_rho4.wait_recv()
    clear_outside(rho0, l0, 5, sizes, (4, 5))
    face_coefficients(rho0, co0, l0, 4, 2.0, 5, (4, 5))
    other_coefficients(rho0, co0, l0, 4, 2.0, 2)
    fine_r.wait_recv()
    fine_r.wait_send()
    begin(r0, co0[4], d01, l0, 4, first, 4)
    smooth(d01, r0, d02, co0, l0, 3, *pairs[0], 9)
    smooth(d02, r0, d03, co0, l0, 2, *pairs[1], 8)
    smooth(d03, r0, d04, co0, l0, 1, *pairs[2], 7)

    def finish_down0(i, ys, here, applied):
        up0[i, :, ys, :] = r0[i, :, ys, :] - applied
        x0[i, :, ys, :] = (d01[i, :, ys, :] + d02[i, :, ys, :]) + (d03[i, :, ys, :] + here)

    sweep(d04, co0, l0, 0, 6, finish_down0)

    restricted(up0, r1, l0, l1)
    second = sender.exchange(sender.group(), r1, l1, 4, AROUND)
    density2.wait_recv()
    density2x = sender.exchange(sender.group(), rho2, l2, 8, line_x2, whole_y=True)
    back0 = sender.exchange(sender.group(), up0, l0, 4, AROUND)
    density1.wait_recv()
    density1.wait_send()
    clear_outside(rho1, l1, 7, sizes)
    coefficients(rho1, co1, l1, 6, 0.5, 2)
    second.wait_recv()
    second.wait_send()
    begin(r1, co1[4], d11, l1, 4, first, 7)
    smooth(d11, r1, d12, co1, l1, 3, *pairs[0], 12)
    smooth(d12, r1, d13, co1, l1, 2, *pairs[1], 10)
    smooth(d13, r1, d14, co1, l1, 1, *pairs[2], 8)

    def finish_down1(i, ys, here, applied):
        up1[i, :, ys, :] = r1[i, :, ys, :] - applied
        x1[i, :, ys, :] = (d11[i, :, ys, :] + d12[i, :, ys, :]) + (d13[i, :, ys, :] + here)

    sweep(d14, co1, l1, 0, 6, finish_down1)

    restricted(up1, r2, l1, l2)
    third = sender.exchange(sender.group(), r2, l2, 7, coarse_offsets)
    back1 = sender.exchange(sender.group(), up1, l1, 6, AROUND)
    sender.exchange(back1, x1, l1, 3, AROUND)
    density2x.wait_recv()
    density2.wait_send()
    density2x.wait_send()
    clear_outside(rho2, l2, 8, sizes)
    coefficients(rho2, co2, l2, 7, 0.125, 2)
    third.wait_recv()
    third.wait_send()
    begin(r2, co2[4], d21, l2, 7, first2, 17)

    def copy_total(i, c):
        x2[i, :, l2["h"] : l2["h"] + 3, :] = d21[i, :, l2["h"] : l2["h"] + 3, :]
        return c

    columns(l2["h"], l2["h"] + 3, 3, copy_total, 0)
    v, d = d21, d22
    for k, (alpha, beta) in enumerate(pairs2):
        smooth(v, r2, d, co2, l2, 6 - k, alpha, beta, 15)
        v, d = d, v

        def add_total(i, c, v=v):
            x2[i, :, l2["h"] : l2["h"] + 3, :] = x2[i, :, l2["h"] : l2["h"] + 3, :] + v[i, :, l2["h"] : l2["h"] + 3, :]
            return c

        columns(l2["h"], l2["h"] + 3, 3, add_total, 0)

    fourth = sender.exchange(sender.group(), x2, l2, 4, diamond(3, 4, 2))
    back1.wait_recv()
    back1.wait_send()
    fourth.wait_recv()
    clear_outside(x2, l2, 4, sizes)
    prolonged(x2, u1, l2, l1, 4)
    smooth(u1, up1, d11, co1, l1, 6, None, first, 9)
    smooth(d11, up1, d12, co1, l1, 5, *pairs[0], 8)
    smooth(d12, up1, d13, co1, l1, 4, *pairs[1], 14)
    smooth(d13, up1, d14, co1, l1, 3, *pairs[2], 12)
    reach1 = pl.ds(l1["h"] - 3, 12)

    def finish_up1(i, c):
        total = (x1[i, :, reach1, :] + u1[i, :, reach1, :]) + (d11[i, :, reach1, :] + d12[i, :, reach1, :])
        x1[i, :, reach1, :] = total + (d13[i, :, reach1, :] + d14[i, :, reach1, :])
        return c

    columns(l1["h"] - 3, l1["h"] + 9, 6, finish_up1, 0)
    clear_outside(x1, l1, 3, sizes)

    prolonged(x1, u0, l1, l0, 3)
    back0.wait_recv()
    back0.wait_send()
    smooth(u0, up0, d01, co0, l0, 4, None, first, 10)
    smooth(d01, up0, d02, co0, l0, 3, *pairs[0], 9)
    smooth(d02, up0, d03, co0, l0, 2, *pairs[1], 8)
    smooth(d03, up0, d04, co0, l0, 1, *pairs[2], 7)

    def finish_up0(i, ys, here, applied):
        j = i - l0["h"]
        total = (x0[i, :, ys, :] + u0[i, :, ys, :]) + (d01[i, :, ys, :] + d02[i, :, ys, :])
        total = total + (d03[i, :, ys, :] + here)
        rest = up0[i, :, ys, :] - applied
        for t in range(4):
            out_x[j, :, 128 * t : 128 * t + 128] = total[t]
            out_r[j, :, 128 * t : 128 * t + 128] = rest[t]

    sweep(d04, co0, l0, 0, 6, finish_up0)
    pl.when(has_above)(upwards.wait_send)
    pl.when(has_below)(downwards.wait_send)
    fine_rho.wait_send()
    fine_rho4.wait_send()
    fourth.wait_send()


GROUPS = 13


def per_device(sizes, right_side, phase):
    def field(level):
        return pltpu.VMEM((level["cols"], level["t"], level["rows"], 128), jnp.float32)

    l0, l1, l2 = LEVELS
    shape = right_side.shape
    result = pltpu.VMEM(shape, jnp.float32)
    whole = pl.BlockSpec(memory_space=pltpu.VMEM)
    return pl.pallas_call(
        functools.partial(kernel, sizes),
        out_shape=(result, result),
        in_specs=[pl.BlockSpec(memory_space=pl.ANY)] * 2,
        out_specs=(whole, whole),
        scratch_shapes=[field(l0)] * 14
        + [field(l1)] * 14
        + [field(l2)] * 10
        + [pltpu.VMEM(shape, jnp.int32)]
        + [pltpu.VMEM((12, 16, 128), jnp.float32)] * 4
        + [pltpu.VMEM((1280, 128), jnp.float32)]
        + [pltpu.SemaphoreType.DMA((5,))]
        + [pltpu.SemaphoreType.DMA((GROUPS,))] * 2,
        compiler_params=pltpu.CompilerParams(
            collective_id=0, has_side_effects=True, vmem_limit_bytes=56 * 1024 * 1024
        ),
        cost_estimate=pl.CostEstimate(flops=60_000_000, bytes_accessed=1_200_000, transcendentals=0),
        name="cycle",
    )(right_side, phase)


def solution(mesh):
    spec = P("gx", "gy", "gz")
    return jax.shard_map(
        functools.partial(per_device, dict(mesh.shape)),
        mesh=mesh,
        in_specs=(spec, spec),
        out_specs=(spec, spec),
        check_vma=False,
    )
```

```python
import functools

import jax
import jax.numpy as jnp
from jax import lax
from jax.experimental import pallas as pl
from jax.experimental.pallas import tpu as pltpu
from jax.sharding import PartitionSpec as P

MESH = pl.DeviceIdType.MESH
DEGREE = 4
COARSE_ITERS = 8
HEAVY = 20.0
SMOOTH_LOWEST = 0.3
COARSE_LOWEST = 0.02
UPPER = 2.0

LEVELS = (
    dict(n=12, h=6, t=5, cols=24, rows=32),
    dict(n=6, h=8, t=3, cols=22, rows=32),
    dict(n=3, h=8, t=2, cols=19, rows=32),
)


def weights(lowest, degree):
    middle, radius = (UPPER + lowest) / 2.0, (UPPER - lowest) / 2.0
    sharpness = middle / radius
    old = 1.0 / sharpness
    pairs = []
    for _ in range(1, degree):
        new = 1.0 / (2.0 * sharpness - old)
        pairs.append((new * old, 2.0 * new / radius))
        old = new
    return 1.0 / middle, pairs


def columns(lo, hi, unroll, body, carry):
    trips = (hi - lo) // unroll

    def several(k, c):
        for j in range(unroll):
            c = body(lo + k * unroll + j, c)
        return c

    if trips > 1:
        carry = lax.fori_loop(0, trips, several, carry)
    elif trips == 1:
        carry = several(0, carry)
    for i in range(lo + trips * unroll, hi):
        carry = body(i, carry)
    return carry


def lanes(shape):
    return lax.broadcasted_iota(jnp.int32, shape, len(shape) - 1)


def shifted(blocks, towards):
    count = len(blocks)
    shape = blocks[0].shape
    edge = lanes(shape) == (127 if towards > 0 else 0)
    rolled = [pltpu.roll(v, 127 if towards > 0 else 1, 1) for v in blocks]
    return [jnp.where(edge, rolled[(t + towards) % count], rolled[t]) for t in range(count)]


def split(block):
    return [block[t] for t in range(block.shape[0])]


def picked(value, index):
    return jnp.take_along_axis(value, index, axis=1)


def halved(blocks):
    lane = lanes(blocks[0].shape)
    index = (2 * lane) % 128
    pairs = [picked(v + pltpu.roll(v, 127, 1), index) for v in blocks]
    out = [jnp.where(lane < 64, pairs[2 * t], pairs[2 * t + 1]) for t in range(len(blocks) // 2)]
    out.append(pairs[-1])
    return out


def doubled(blocks):
    lane = lanes(blocks[0].shape)
    low, high = lane // 2, 64 + lane // 2
    out = []
    for v in blocks[:-1]:
        out += [picked(v, low), picked(v, high)]
    out.append(picked(blocks[-1], jnp.where(lane < 64, low, high)))
    return out


def near(o, n):
    return (abs(o) - 1) * n + 1 if o else 0


def reach(offset, n, w):
    return max(offset * n, -w), min(offset * n + n, n + w)


class Group:
    def __init__(self, send_sem, recv_sem, blank):
        self.send, self.recv, self.blank, self.count = send_sem, recv_sem, blank, 0

    def wait(self, sem):
        rows = self.blank.at[0 : self.count, :]
        pltpu.make_async_copy(rows, rows, sem).wait()

    def wait_recv(self):
        self.wait(self.recv)

    def wait_send(self):
        self.wait(self.send)


class Sender:
    def __init__(self, send_sems, recv_sems, blank, sizes):
        self.send, self.recv, self.blank, self.sizes = send_sems, recv_sems, blank, sizes
        self.groups = []

    def target(self, offset):
        place = []
        for axis, o in zip(("gx", "gy", "gz"), offset):
            size = self.sizes[axis]
            place.append(lax.rem(lax.axis_index(axis) + (o + 4 * size), size) if o else lax.axis_index(axis))
        return tuple(place)

    def group(self):
        k = len(self.groups)
        self.groups.append(Group(self.send.at[k], self.recv.at[k], self.blank))
        return self.groups[-1]

    def start(self, group, src, dst, offset):
        copy = pltpu.make_async_remote_copy(
            src_ref=src,
            dst_ref=dst,
            send_sem=group.send,
            recv_sem=group.recv,
            device_id=self.target(offset),
            device_id_type=MESH,
        )
        copy.start()

    def exchange(self, group, ref, level, w, offsets, tiles=None, whole_y=False, zeros=None, cut=False):
        n, h = level["n"], level["h"]
        t0, t1 = tiles or (0, level["t"])
        for ox, oy in offsets:
            spans = [(reach(ox, n, w - near(oy, n)), (-w, n + w) if whole_y else reach(oy, n, w - near(ox, n)))]
            if cut and ox and oy:
                low, high = reach(ox, n, 2), reach(ox, n, w - 1)
                rest = (high[0], low[0]) if ox < 0 else (low[1], high[1])
                spans = [(low, reach(oy, n, w - 1)), (rest, reach(oy, n, w - 3))]
            for (x0, x1), (y0, y1) in spans:
                self.block(group, ref, (x1 - x0, t0, t1, y1 - y0), (x0, y0), (ox * n, oy * n), h, (-ox, -oy, 0), zeros)
        return group

    def block(self, group, ref, shape, corner, shift, h, offset, zeros):
        x, t0, t1, y = shape
        dx, dy = corner[0] + h, corner[1] + h
        sx, sy = dx - shift[0], dy - shift[1]
        dst = ref.at[dx : dx + x, t0:t1, dy : dy + y, :]

        def send(src):
            self.start(group, src, dst, offset)

        group.count += x * (t1 - t0) * y
        src = ref.at[sx : sx + x, t0:t1, sy : sy + y, :]
        if zeros is None:
            send(src)
            return
        outside = None
        for axis, o in zip(("gx", "gy"), offset):
            if o:
                place = lax.axis_index(axis) + o
                beyond = place < 0 if o < 0 else place >= self.sizes[axis]
                outside = beyond if outside is None else jnp.logical_or(outside, beyond)
        pl.when(outside)(lambda: send(zeros.at[0:x, 0 : t1 - t0, 0:y, :]))
        pl.when(jnp.logical_not(outside))(lambda: send(src))


def diamond(n, w, most):
    found = []
    for ox in range(-most, most + 1):
        for oy in range(-most, most + 1):
            if (ox or oy) and near(ox, n) + near(oy, n) <= w:
                found.append((ox, oy))
    return sorted(found, key=lambda o: -abs(o[0]) - abs(o[1]))


AROUND = diamond(1, 2, 1)
FACES = [o for o in AROUND if 0 in o]
CORNERS = [o for o in AROUND if 0 not in o]


def inverse_of(value):
    guess = pl.reciprocal(value, approx=True)
    return guess * (2.0 - value * guess)


def conduct(a, b, scale):
    return scale * inverse_of(jnp.maximum(a + b, 0.5))


def face_coefficients(rho, co, level, w, scale, unroll, tiles=None):
    bx, by = co[:2]
    n, h = level["n"], level["h"]
    lo, hi, rows = h - w, h + n + w, n + 2 * w
    ts, ys, ends = slice(*(tiles or (0, level["t"]))), pl.ds(lo, rows), pl.ds(lo - 1, rows + 1)

    def body(i, c):
        bx[i, ts, ys, :] = conduct(rho[i, ts, ys, :], rho[i + 1, ts, ys, :], scale)
        by[i, ts, ends, :] = conduct(rho[i, ts, ends, :], rho[i, ts, pl.ds(lo, rows + 1), :], scale)
        return c

    bx[lo - 1, ts, ys, :] = conduct(rho[lo - 1, ts, ys, :], rho[lo, ts, ys, :], scale)
    columns(lo, hi, unroll, body, 0)


def other_coefficients(rho, co, level, w, scale, unroll):
    bx, by, bzp, bzm, iv = co
    n, h = level["n"], level["h"]
    lo, hi, rows = h - w, h + n + w, n + 2 * w
    ys = pl.ds(lo, rows)

    def body(i, c):
        here = rho[i, :, ys, :]
        above = jnp.stack([conduct(a, b, scale) for a, b in zip(split(here), shifted(split(here), 1))])
        below = jnp.stack(shifted(split(above), -1))
        bzp[i, :, ys, :] = above
        bzm[i, :, ys, :] = below
        total = (bx[i - 1, :, ys, :] + bx[i, :, ys, :]) + (by[i, :, ys, :] + by[i, :, pl.ds(lo - 1, rows), :])
        iv[i, :, ys, :] = jnp.where(here > 0.0, inverse_of(total + (above + below)), 0.0)
        return c

    columns(lo, hi, unroll, body, 0)


def coefficients(rho, co, level, w, scale, unroll):
    face_coefficients(rho, co, level, w, scale, unroll)
    other_coefficients(rho, co, level, w, scale, unroll)


def begin(r, iv, d, level, w, weight, unroll):
    n, h = level["n"], level["h"]
    ys = pl.ds(h - w, n + 2 * w)

    def body(i, c):
        d[i, :, ys, :] = weight * (iv[i, :, ys, :] * r[i, :, ys, :])
        return c

    columns(h - w, h + n + w, unroll, body, 0)


def sweep(v, co, level, w, unroll, finish, tiles=None):
    bx, by, bzp, bzm, _ = co
    n, h, t = level["n"], level["h"], level["t"]
    lo, hi, rows = h - w, h + n + w, n + 2 * w
    ys, up, down = pl.ds(lo, rows), pl.ds(lo + 1, rows), pl.ds(lo - 1, rows)

    def body(i, carry):
        here, before = carry
        after = v[i + 1, :, ys, :]
        flux = bx[i, :, ys, :] * (here - after)
        parts = split(here)
        zp = jnp.stack(shifted(parts, 1))
        zm = jnp.stack(shifted(parts, -1))
        total = (flux - before) + bzp[i, :, ys, :] * (here - zp) + bzm[i, :, ys, :] * (here - zm)
        total = total + by[i, :, ys, :] * (here - v[i, :, up, :])
        total = total + by[i, :, down, :] * (here - v[i, :, down, :])
        finish(i, ys, here, total)
        return after, flux

    here = v[lo, :, ys, :]
    before = bx[lo - 1, :, ys, :] * (v[lo - 1, :, ys, :] - here)
    columns(lo, hi, unroll, body, (here, before))


def smooth(v, r, d, co, level, w, alpha, beta, unroll, total=None):
    iv = co[4]

    def finish(i, ys, here, applied):
        rest = r[i, :, ys, :] - applied
        r[i, :, ys, :] = rest
        new = beta * (iv[i, :, ys, :] * rest)
        if alpha is not None:
            new = alpha * here + new
        d[i, :, ys, :] = new
        if total is not None:
            total[i, :, ys, :] = total[i, :, ys, :] + new

    sweep(v, co, level, w, unroll, finish)


def restricted(fine, coarse, level_fine, level_coarse):
    h, n, hc = level_fine["h"], level_coarse["n"], level_coarse["h"]

    def body(i, c):
        x = h + 2 * i
        even, odd = pl.ds(h, n, stride=2), pl.ds(h + 1, n, stride=2)
        blocks = []
        for t in range(level_fine["t"]):
            both = fine[x, t, even, :] + fine[x, t, odd, :]
            both = both + (fine[x + 1, t, even, :] + fine[x + 1, t, odd, :])
            blocks.append(both)
        coarse[hc + i, :, hc : hc + n, :] = jnp.stack(halved(blocks)) * 0.125
        return c

    for i in range(n):
        body(i, 0)


def prolonged(coarse, fine, level_coarse, level_fine, w):
    hc, h, n = level_coarse["h"], level_fine["h"], level_coarse["n"]
    count = n + 2 * w

    def body(k, c):
        block = doubled(split(coarse[hc - w + k, :, hc - w : hc - w + count, :]))
        for t, v in enumerate(block):
            for x in (0, 1):
                for y in (0, 1):
                    fine[h - 2 * w + 2 * k + x, t, pl.ds(h - 2 * w + y, count, stride=2), :] = v
        return c

    columns(0, count, 6, body, 0)


def kernel(sizes, rhs, phase, out, *scratch):
    scratch = list(scratch)

    def take(count):
        taken, scratch[:count] = scratch[:count], []
        return taken

    rho0, r0, up0, u0, x0, d01, d02, d03, d04 = take(9)
    co0 = take(5)
    rho1, r1, up1, u1, x1, d11, d12, d13, d14 = take(9)
    co1 = take(5)
    rho2, r2, x2, d21, d22 = take(5)
    co2 = take(5)
    kind, zs_up, zs_down, zr_below, zr_above, blank, zeros, local_sems, send_sems, recv_sems = take(10)
    l0, l1, l2 = LEVELS
    sender = Sender(send_sems, recv_sems, blank, sizes)
    first, pairs = weights(SMOOTH_LOWEST, DEGREE)
    first2, pairs2 = weights(COARSE_LOWEST, COARSE_ITERS)
    own = slice(l0["h"], l0["h"] + 12)

    loads = [pltpu.make_async_copy(phase, kind, local_sems.at[4])]
    for t in range(4):
        loads.append(
            pltpu.make_async_copy(rhs.at[:, :, 128 * t : 128 * t + 128], r0.at[own, t, own, :], local_sems.at[t])
        )
    for copy in loads:
        copy.start()

    coarse_offsets = diamond(3, 7, 3)
    line_y2 = [(0, o) for o in (3, -3, 2, -2, 1, -1)]
    line_x2 = [(o, 0) for _, o in line_y2]
    met = sorted({(ox, oy, 0) for ox, oy in coarse_offsets + line_y2 + line_x2 + AROUND})
    gz = lax.axis_index("gz")
    has_below, has_above = gz > 0, gz < sizes["gz"] - 1
    barrier = pltpu.get_barrier_semaphore()

    def greet(offset):
        pl.semaphore_signal(barrier, inc=1, device_id=sender.target(offset), device_id_type=MESH)

    pl.when(has_above)(lambda: greet((0, 0, 1)))
    pl.when(has_below)(lambda: greet((0, 0, -1)))
    for offset in met:
        greet(offset)

    zeros[...] = jnp.zeros_like(zeros)

    lane = lanes((12, 128))
    for copy in loads:
        copy.wait()

    def prepare(i, c):
        x = i + l0["h"]
        density = []
        for t in range(4):
            part = slice(128 * t, 128 * t + 128)
            density.append(jnp.where(kind[i, :, part] == 1, HEAVY, 1.0).astype(jnp.float32))
            rho0[x, t, own, :] = density[t]
        zs_up[i, :12, :] = jnp.where(lane >= 64, r0[x, 3, own, :], pltpu.roll(density[3], 64, 1))
        zs_down[i, :12, :] = jnp.where(lane < 64, r0[x, 0, own, :], pltpu.roll(density[0], 64, 1))
        return c

    columns(0, 12, 4, prepare, 0)
    beside = jnp.where(has_below, 1, 0) + jnp.where(has_above, 1, 0)
    pl.semaphore_wait(barrier, len(met) + beside)

    upwards, downwards = sender.group(), sender.group()
    upwards.count = downwards.count = 12 * 12

    @pl.when(has_above)
    def _():
        sender.start(upwards, zs_up.at[:, :12, :], zr_below.at[:, :12, :], (0, 0, 1))

    @pl.when(has_below)
    def _():
        sender.start(downwards, zs_down.at[:, :12, :], zr_above.at[:, :12, :], (0, 0, -1))

    @pl.when(jnp.logical_not(has_below))
    def _():
        zr_below[...] = jnp.zeros_like(zr_below)

    @pl.when(jnp.logical_not(has_above))
    def _():
        zr_above[...] = jnp.zeros_like(zr_above)

    fine_rho = sender.exchange(sender.group(), rho0, l0, 5, AROUND, (0, 4), zeros=zeros, cut=True)
    fine_r = sender.exchange(sender.group(), r0, l0, 4, FACES, (0, 4))

    pl.when(has_below)(upwards.wait_recv)
    pl.when(has_above)(downwards.wait_recv)
    inside = jnp.where(lane < 64, jnp.where(has_above, 1.0, 0.0), jnp.where(has_below, 1.0, 0.0))

    def ends(i, c):
        below, above = zr_below[i, :12, :], zr_above[i, :12, :]
        r0[i + l0["h"], 4, own, :] = jnp.where(lane < 64, above, below)
        rho0[i + l0["h"], 4, own, :] = inside * pltpu.roll(jnp.where(lane < 64, below, above), 64, 1)
        return c

    columns(0, 12, 6, ends, 0)
    fine_rho4 = sender.exchange(sender.group(), rho0, l0, 5, AROUND, (4, 5), zeros=zeros, cut=True)
    sender.exchange(fine_r, r0, l0, 4, CORNERS, cut=True)
    sender.exchange(fine_r, r0, l0, 4, FACES, (4, 5))

    restricted(rho0, rho1, l0, l1)
    restricted(rho1, rho2, l1, l2)
    density1 = sender.exchange(sender.group(), rho1, l1, 7, diamond(6, 7, 2), zeros=zeros)
    density2 = sender.exchange(sender.group(), rho2, l2, 8, line_y2, zeros=zeros)

    fine_rho.wait_recv()
    face_coefficients(rho0, co0, l0, 4, 2.0, 2, (0, 4))
    fine_rho4.wait_recv()
    face_coefficients(rho0, co0, l0, 4, 2.0, 5, (4, 5))
    other_coefficients(rho0, co0, l0, 4, 2.0, 2)
    fine_r.wait_recv()
    fine_r.wait_send()
    begin(r0, co0[4], d01, l0, 4, first, 4)
    smooth(d01, r0, d02, co0, l0, 3, *pairs[0], 9)
    smooth(d02, r0, d03, co0, l0, 2, *pairs[1], 8)
    smooth(d03, r0, d04, co0, l0, 1, *pairs[2], 7)

    def finish_down0(i, ys, here, applied):
        up0[i, :, ys, :] = r0[i, :, ys, :] - applied
        x0[i, :, ys, :] = (d01[i, :, ys, :] + d02[i, :, ys, :]) + (d03[i, :, ys, :] + here)

    sweep(d04, co0, l0, 0, 6, finish_down0)

    restricted(up0, r1, l0, l1)
    second = sender.exchange(sender.group(), r1, l1, 4, AROUND)
    density2.wait_recv()
    density2x = sender.exchange(sender.group(), rho2, l2, 8, line_x2, whole_y=True, zeros=zeros)
    density1.wait_recv()
    density1.wait_send()
    coefficients(rho1, co1, l1, 6, 0.5, 2)
    back0 = sender.exchange(sender.group(), up0, l0, 4, AROUND)
    second.wait_recv()
    second.wait_send()
    begin(r1, co1[4], d11, l1, 4, first, 7)
    smooth(d11, r1, d12, co1, l1, 3, *pairs[0], 12)
    smooth(d12, r1, d13, co1, l1, 2, *pairs[1], 10)
    smooth(d13, r1, d14, co1, l1, 1, *pairs[2], 8)

    def finish_down1(i, ys, here, applied):
        up1[i, :, ys, :] = r1[i, :, ys, :] - applied
        x1[i, :, ys, :] = (d11[i, :, ys, :] + d12[i, :, ys, :]) + (d13[i, :, ys, :] + here)

    sweep(d14, co1, l1, 0, 6, finish_down1)

    restricted(up1, r2, l1, l2)
    third = sender.exchange(sender.group(), r2, l2, 7, coarse_offsets)
    density2x.wait_recv()
    density2.wait_send()
    density2x.wait_send()
    coefficients(rho2, co2, l2, 7, 0.125, 2)
    back1 = sender.exchange(sender.group(), up1, l1, 6, AROUND)
    sender.exchange(back1, x1, l1, 3, AROUND, zeros=zeros)
    third.wait_recv()
    third.wait_send()
    begin(r2, co2[4], d21, l2, 7, first2, 17)

    def copy_total(i, c):
        x2[i, :, l2["h"] : l2["h"] + 3, :] = d21[i, :, l2["h"] : l2["h"] + 3, :]
        return c

    columns(l2["h"], l2["h"] + 3, 3, copy_total, 0)
    v, d = d21, d22
    for k, (alpha, beta) in enumerate(pairs2):
        smooth(v, r2, d, co2, l2, 6 - k, alpha, beta, 15)
        v, d = d, v

        def add_total(i, c, v=v):
            x2[i, :, l2["h"] : l2["h"] + 3, :] = x2[i, :, l2["h"] : l2["h"] + 3, :] + v[i, :, l2["h"] : l2["h"] + 3, :]
            return c

        columns(l2["h"], l2["h"] + 3, 3, add_total, 0)

    fourth = sender.exchange(sender.group(), x2, l2, 4, diamond(3, 4, 2), zeros=zeros)
    back1.wait_recv()
    back1.wait_send()
    fourth.wait_recv()
    prolonged(x2, u1, l2, l1, 4)
    smooth(u1, up1, d11, co1, l1, 6, None, first, 9)
    smooth(d11, up1, d12, co1, l1, 5, *pairs[0], 8)
    smooth(d12, up1, d13, co1, l1, 4, *pairs[1], 14)
    alpha, beta = pairs[2]

    def finish_up1(i, ys, here, applied):
        new = alpha * here + beta * (co1[4][i, :, ys, :] * (up1[i, :, ys, :] - applied))
        total = (x1[i, :, ys, :] + u1[i, :, ys, :]) + (d11[i, :, ys, :] + d12[i, :, ys, :])
        x1[i, :, ys, :] = total + (here + new)

    sweep(d13, co1, l1, 3, 12, finish_up1)

    prolonged(x1, u0, l1, l0, 3)
    back0.wait_recv()
    back0.wait_send()
    smooth(u0, up0, d01, co0, l0, 4, None, first, 10)
    smooth(d01, up0, d02, co0, l0, 3, *pairs[0], 9)
    smooth(d02, up0, d03, co0, l0, 2, *pairs[1], 8)
    smooth(d03, up0, d04, co0, l0, 1, *pairs[2], 7)

    def finish_up0(i, ys, here, applied):
        j = i - l0["h"]
        total = (x0[i, :, ys, :] + u0[i, :, ys, :]) + (d01[i, :, ys, :] + d02[i, :, ys, :])
        total = total + (d03[i, :, ys, :] + here)
        rest = up0[i, :, ys, :] - applied
        for t in range(4):
            out[0, j, :, 128 * t : 128 * t + 128] = total[t]
            out[1, j, :, 128 * t : 128 * t + 128] = rest[t]

    sweep(d04, co0, l0, 0, 6, finish_up0)
    pl.when(has_above)(upwards.wait_send)
    pl.when(has_below)(downwards.wait_send)
    fine_rho.wait_send()
    fine_rho4.wait_send()
    fourth.wait_send()


GROUPS = 13


def per_device(sizes, right_side, phase):
    def field(level):
        return pltpu.VMEM((level["cols"], level["t"], level["rows"], 128), jnp.float32)

    l0, l1, l2 = LEVELS
    shape = right_side.shape
    result = pltpu.VMEM(shape, jnp.float32)
    whole = pl.BlockSpec(memory_space=pltpu.VMEM)
    both = pl.pallas_call(
        functools.partial(kernel, sizes),
        out_shape=pltpu.VMEM((2,) + shape, jnp.float32),
        in_specs=[pl.BlockSpec(memory_space=pl.ANY)] * 2,
        out_specs=whole,
        scratch_shapes=[field(l0)] * 14
        + [field(l1)] * 14
        + [field(l2)] * 10
        + [pltpu.VMEM(shape, jnp.int32)]
        + [pltpu.VMEM((12, 16, 128), jnp.float32)] * 4
        + [pltpu.VMEM((1280, 128), jnp.float32), pltpu.VMEM((12, 4, 24, 128), jnp.float32)]
        + [pltpu.SemaphoreType.DMA((5,))]
        + [pltpu.SemaphoreType.DMA((GROUPS,))] * 2,
        compiler_params=pltpu.CompilerParams(
            collective_id=0, has_side_effects=True, vmem_limit_bytes=56 * 1024 * 1024
        ),
        cost_estimate=pl.CostEstimate(flops=60_000_000, bytes_accessed=1_200_000, transcendentals=0),
        name="cycle",
    )(right_side, phase)
    return both[0], both[1]


def solution(mesh):
    spec = P("gx", "gy", "gz")
    return jax.shard_map(
        functools.partial(per_device, dict(mesh.shape)),
        mesh=mesh,
        in_specs=(spec, spec),
        out_specs=(spec, spec),
        check_vma=False,
    )
```

```python
import functools

import jax
import jax.numpy as jnp
from jax import lax
from jax.experimental import pallas as pl
from jax.experimental.pallas import tpu as pltpu
from jax.sharding import PartitionSpec as P

MESH = pl.DeviceIdType.MESH
DEGREE = 4
COARSE_ITERS = 8
HEAVY = 20.0
SMOOTH_LOWEST = 0.3
COARSE_LOWEST = 0.02
UPPER = 2.0

LEVELS = (
    dict(n=12, h=6, t=5, cols=24, rows=32),
    dict(n=6, h=8, t=3, cols=22, rows=32),
    dict(n=3, h=8, t=2, cols=19, rows=32),
)


def weights(lowest, degree):
    middle, radius = (UPPER + lowest) / 2.0, (UPPER - lowest) / 2.0
    sharpness = middle / radius
    old = 1.0 / sharpness
    pairs = []
    for _ in range(1, degree):
        new = 1.0 / (2.0 * sharpness - old)
        pairs.append((new * old, 2.0 * new / radius))
        old = new
    return 1.0 / middle, pairs


def columns(lo, hi, unroll, body, carry):
    trips = (hi - lo) // unroll

    def several(k, c):
        for j in range(unroll):
            c = body(lo + k * unroll + j, c)
        return c

    if trips > 1:
        carry = lax.fori_loop(0, trips, several, carry)
    elif trips == 1:
        carry = several(0, carry)
    for i in range(lo + trips * unroll, hi):
        carry = body(i, carry)
    return carry


def lanes(shape):
    return lax.broadcasted_iota(jnp.int32, shape, len(shape) - 1)


def shifted(blocks, towards):
    count = len(blocks)
    shape = blocks[0].shape
    edge = lanes(shape) == (127 if towards > 0 else 0)
    rolled = [pltpu.roll(v, 127 if towards > 0 else 1, 1) for v in blocks]
    return [jnp.where(edge, rolled[(t + towards) % count], rolled[t]) for t in range(count)]


def split(block):
    return [block[t] for t in range(block.shape[0])]


def picked(value, index):
    return jnp.take_along_axis(value, index, axis=1)


def halved(blocks):
    lane = lanes(blocks[0].shape)
    index = (2 * lane) % 128
    pairs = [picked(v + pltpu.roll(v, 127, 1), index) for v in blocks]
    out = [jnp.where(lane < 64, pairs[2 * t], pairs[2 * t + 1]) for t in range(len(blocks) // 2)]
    out.append(pairs[-1])
    return out


def doubled(blocks):
    lane = lanes(blocks[0].shape)
    low, high = lane // 2, 64 + lane // 2
    out = []
    for v in blocks[:-1]:
        out += [picked(v, low), picked(v, high)]
    out.append(picked(blocks[-1], jnp.where(lane < 64, low, high)))
    return out


def near(o, n):
    return (abs(o) - 1) * n + 1 if o else 0


def reach(offset, n, w):
    return max(offset * n, -w), min(offset * n + n, n + w)


class Group:
    def __init__(self, send_sem, recv_sem, blank):
        self.send, self.recv, self.blank, self.count = send_sem, recv_sem, blank, 0

    def wait(self, sem):
        rows = self.blank.at[0 : self.count, :]
        pltpu.make_async_copy(rows, rows, sem).wait()

    def wait_recv(self):
        self.wait(self.recv)

    def wait_send(self):
        self.wait(self.send)


class Sender:
    def __init__(self, send_sems, recv_sems, blank, sizes):
        self.send, self.recv, self.blank, self.sizes = send_sems, recv_sems, blank, sizes
        self.groups = []

    def target(self, offset):
        place = []
        for axis, o in zip(("gx", "gy", "gz"), offset):
            size = self.sizes[axis]
            place.append(lax.rem(lax.axis_index(axis) + (o + 4 * size), size) if o else lax.axis_index(axis))
        return tuple(place)

    def group(self):
        k = len(self.groups)
        self.groups.append(Group(self.send.at[k], self.recv.at[k], self.blank))
        return self.groups[-1]

    def start(self, group, src, dst, offset):
        copy = pltpu.make_async_remote_copy(
            src_ref=src,
            dst_ref=dst,
            send_sem=group.send,
            recv_sem=group.recv,
            device_id=self.target(offset),
            device_id_type=MESH,
        )
        copy.start()

    def exchange(self, group, ref, level, w, offsets, tiles=None, whole_y=False, zeros=None, cut=False):
        n, h = level["n"], level["h"]
        t0, t1 = tiles or (0, level["t"])
        for ox, oy in offsets:
            spans = [(reach(ox, n, w - near(oy, n)), (-w, n + w) if whole_y else reach(oy, n, w - near(ox, n)))]
            if cut and ox and oy:
                low, high = reach(ox, n, 2), reach(ox, n, w - 1)
                rest = (high[0], low[0]) if ox < 0 else (low[1], high[1])
                spans = [(low, reach(oy, n, w - 1)), (rest, reach(oy, n, w - 3))]
            for (x0, x1), (y0, y1) in spans:
                self.block(group, ref, (x1 - x0, t0, t1, y1 - y0), (x0, y0), (ox * n, oy * n), h, (-ox, -oy, 0), zeros)
        return group

    def block(self, group, ref, shape, corner, shift, h, offset, zeros):
        x, t0, t1, y = shape
        dx, dy = corner[0] + h, corner[1] + h
        sx, sy = dx - shift[0], dy - shift[1]
        dst = ref.at[dx : dx + x, t0:t1, dy : dy + y, :]

        def send(src):
            self.start(group, src, dst, offset)

        group.count += x * (t1 - t0) * y
        src = ref.at[sx : sx + x, t0:t1, sy : sy + y, :]
        if zeros is None:
            send(src)
            return
        outside = None
        for axis, o in zip(("gx", "gy"), offset):
            if o:
                place = lax.axis_index(axis) + o
                beyond = place < 0 if o < 0 else place >= self.sizes[axis]
                outside = beyond if outside is None else jnp.logical_or(outside, beyond)
        pl.when(outside)(lambda: send(zeros.at[0:x, 0 : t1 - t0, 0:y, :]))
        pl.when(jnp.logical_not(outside))(lambda: send(src))


def diamond(n, w, most):
    found = []
    for ox in range(-most, most + 1):
        for oy in range(-most, most + 1):
            if (ox or oy) and near(ox, n) + near(oy, n) <= w:
                found.append((ox, oy))
    return sorted(found, key=lambda o: -abs(o[0]) - abs(o[1]))


AROUND = diamond(1, 2, 1)
FACES = [o for o in AROUND if 0 in o]
CORNERS = [o for o in AROUND if 0 not in o]


def inverse_of(value):
    guess = pl.reciprocal(value, approx=True)
    return guess * (2.0 - value * guess)


def conduct(a, b):
    return inverse_of(jnp.maximum(a + b, 0.25))


def face_coefficients(rho, co, level, w, unroll, tiles=None):
    bx, by = co[:2]
    n, h = level["n"], level["h"]
    lo, hi, rows = h - w, h + n + w, n + 2 * w
    ts, ys, ends = slice(*(tiles or (0, level["t"]))), pl.ds(lo, rows), pl.ds(lo - 1, rows + 1)

    def body(i, c):
        bx[i, ts, ys, :] = conduct(rho[i, ts, ys, :], rho[i + 1, ts, ys, :])
        by[i, ts, ends, :] = conduct(rho[i, ts, ends, :], rho[i, ts, pl.ds(lo, rows + 1), :])
        return c

    bx[lo - 1, ts, ys, :] = conduct(rho[lo - 1, ts, ys, :], rho[lo, ts, ys, :])
    columns(lo, hi, unroll, body, 0)


def other_coefficients(rho, co, level, w, unroll):
    bx, by, bzp, bzm, iv = co
    n, h = level["n"], level["h"]
    lo, hi, rows = h - w, h + n + w, n + 2 * w
    ys = pl.ds(lo, rows)

    def body(i, c):
        here = rho[i, :, ys, :]
        above = jnp.stack([conduct(a, b) for a, b in zip(split(here), shifted(split(here), 1))])
        below = jnp.stack(shifted(split(above), -1))
        bzp[i, :, ys, :] = above
        bzm[i, :, ys, :] = below
        total = (bx[i - 1, :, ys, :] + bx[i, :, ys, :]) + (by[i, :, ys, :] + by[i, :, pl.ds(lo - 1, rows), :])
        iv[i, :, ys, :] = jnp.where(here > 0.0, inverse_of(total + (above + below)), 0.0)
        return c

    columns(lo, hi, unroll, body, 0)


def coefficients(rho, co, level, w, unroll):
    face_coefficients(rho, co, level, w, unroll)
    other_coefficients(rho, co, level, w, unroll)


def begin(r, iv, d, level, w, weight, unroll):
    n, h = level["n"], level["h"]
    ys = pl.ds(h - w, n + 2 * w)

    def body(i, c):
        d[i, :, ys, :] = weight * (iv[i, :, ys, :] * r[i, :, ys, :])
        return c

    columns(h - w, h + n + w, unroll, body, 0)


def sweep(v, co, level, w, unroll, finish, tiles=None):
    bx, by, bzp, bzm, _ = co
    n, h, t = level["n"], level["h"], level["t"]
    lo, hi, rows = h - w, h + n + w, n + 2 * w
    ys, up, down = pl.ds(lo, rows), pl.ds(lo + 1, rows), pl.ds(lo - 1, rows)

    def body(i, carry):
        here, before = carry
        after = v[i + 1, :, ys, :]
        flux = bx[i, :, ys, :] * (here - after)
        parts = split(here)
        zp = jnp.stack(shifted(parts, 1))
        zm = jnp.stack(shifted(parts, -1))
        total = (flux - before) + bzp[i, :, ys, :] * (here - zp) + bzm[i, :, ys, :] * (here - zm)
        total = total + by[i, :, ys, :] * (here - v[i, :, up, :])
        total = total + by[i, :, down, :] * (here - v[i, :, down, :])
        finish(i, ys, here, total)
        return after, flux

    here = v[lo, :, ys, :]
    before = bx[lo - 1, :, ys, :] * (v[lo - 1, :, ys, :] - here)
    columns(lo, hi, unroll, body, (here, before))


def smooth(v, r, d, co, level, w, alpha, beta, unroll, total=None):
    iv = co[4]

    def finish(i, ys, here, applied):
        rest = r[i, :, ys, :] - applied
        r[i, :, ys, :] = rest
        new = beta * (iv[i, :, ys, :] * rest)
        if alpha is not None:
            new = alpha * here + new
        d[i, :, ys, :] = new
        if total is not None:
            total[i, :, ys, :] = total[i, :, ys, :] + new

    sweep(v, co, level, w, unroll, finish)


def restricted(fine, coarse, level_fine, level_coarse, scale=0.125):
    h, n, hc = level_fine["h"], level_coarse["n"], level_coarse["h"]

    def body(i, c):
        x = h + 2 * i
        even, odd = pl.ds(h, n, stride=2), pl.ds(h + 1, n, stride=2)
        blocks = []
        for t in range(level_fine["t"]):
            both = fine[x, t, even, :] + fine[x, t, odd, :]
            both = both + (fine[x + 1, t, even, :] + fine[x + 1, t, odd, :])
            blocks.append(both)
        coarse[hc + i, :, hc : hc + n, :] = jnp.stack(halved(blocks)) * scale
        return c

    for i in range(n):
        body(i, 0)


def prolonged(coarse, fine, level_coarse, level_fine, w):
    hc, h, n = level_coarse["h"], level_fine["h"], level_coarse["n"]
    count = n + 2 * w

    def body(k, c):
        block = doubled(split(coarse[hc - w + k, :, hc - w : hc - w + count, :]))
        for t, v in enumerate(block):
            for x in (0, 1):
                for y in (0, 1):
                    fine[h - 2 * w + 2 * k + x, t, pl.ds(h - 2 * w + y, count, stride=2), :] = v
        return c

    columns(0, count, 6, body, 0)


def kernel(sizes, rhs, phase, out, *scratch):
    scratch = list(scratch)

    def take(count):
        taken, scratch[:count] = scratch[:count], []
        return taken

    rho0, r0, up0, u0, x0, d01, d02, d03, d04 = take(9)
    co0 = take(5)
    rho1, r1, up1, u1, x1, d11, d12, d13, d14 = take(9)
    co1 = take(5)
    rho2, r2, x2, d21, d22 = take(5)
    co2 = take(5)
    kind, zs_up, zs_down, zr_below, zr_above, blank, zeros, local_sems, send_sems, recv_sems = take(10)
    l0, l1, l2 = LEVELS
    sender = Sender(send_sems, recv_sems, blank, sizes)
    first, pairs = weights(SMOOTH_LOWEST, DEGREE)
    first2, pairs2 = weights(COARSE_LOWEST, COARSE_ITERS)
    own = slice(l0["h"], l0["h"] + 12)

    loads = [pltpu.make_async_copy(phase, kind, local_sems.at[4])]
    for t in range(4):
        loads.append(
            pltpu.make_async_copy(rhs.at[:, :, 128 * t : 128 * t + 128], r0.at[own, t, own, :], local_sems.at[t])
        )
    for copy in loads:
        copy.start()

    coarse_offsets = diamond(3, 7, 3)
    line_y2 = [(0, o) for o in (3, -3, 2, -2, 1, -1)]
    line_x2 = [(o, 0) for _, o in line_y2]
    met = sorted({(ox, oy, 0) for ox, oy in coarse_offsets + line_y2 + line_x2 + AROUND})
    gz = lax.axis_index("gz")
    has_below, has_above = gz > 0, gz < sizes["gz"] - 1
    barrier = pltpu.get_barrier_semaphore()

    def greet(offset):
        pl.semaphore_signal(barrier, inc=1, device_id=sender.target(offset), device_id_type=MESH)

    pl.when(has_above)(lambda: greet((0, 0, 1)))
    pl.when(has_below)(lambda: greet((0, 0, -1)))
    for offset in met:
        greet(offset)

    zeros[...] = jnp.zeros_like(zeros)

    lane = lanes((12, 128))
    for copy in loads:
        copy.wait()

    def prepare(i, c):
        x = i + l0["h"]
        density = []
        for t in range(4):
            part = slice(128 * t, 128 * t + 128)
            density.append(jnp.where(kind[i, :, part] == 1, 0.5 * HEAVY, 0.5).astype(jnp.float32))
            rho0[x, t, own, :] = density[t]
        zs_up[i, :12, :] = jnp.where(lane >= 64, r0[x, 3, own, :], pltpu.roll(density[3], 64, 1))
        zs_down[i, :12, :] = jnp.where(lane < 64, r0[x, 0, own, :], pltpu.roll(density[0], 64, 1))
        return c

    columns(0, 12, 4, prepare, 0)
    beside = jnp.where(has_below, 1, 0) + jnp.where(has_above, 1, 0)
    pl.semaphore_wait(barrier, len(met) + beside)

    upwards, downwards = sender.group(), sender.group()
    upwards.count = downwards.count = 12 * 12

    @pl.when(has_above)
    def _():
        sender.start(upwards, zs_up.at[:, :12, :], zr_below.at[:, :12, :], (0, 0, 1))

    @pl.when(has_below)
    def _():
        sender.start(downwards, zs_down.at[:, :12, :], zr_above.at[:, :12, :], (0, 0, -1))

    @pl.when(jnp.logical_not(has_below))
    def _():
        zr_below[...] = jnp.zeros_like(zr_below)

    @pl.when(jnp.logical_not(has_above))
    def _():
        zr_above[...] = jnp.zeros_like(zr_above)

    fine_rho = sender.exchange(sender.group(), rho0, l0, 5, AROUND, (0, 4), zeros=zeros, cut=True)
    fine_r = sender.exchange(sender.group(), r0, l0, 4, FACES, (0, 4))

    pl.when(has_below)(upwards.wait_recv)
    pl.when(has_above)(downwards.wait_recv)
    inside = jnp.where(lane < 64, jnp.where(has_above, 1.0, 0.0), jnp.where(has_below, 1.0, 0.0))

    def ends(i, c):
        below, above = zr_below[i, :12, :], zr_above[i, :12, :]
        r0[i + l0["h"], 4, own, :] = jnp.where(lane < 64, above, below)
        rho0[i + l0["h"], 4, own, :] = inside * pltpu.roll(jnp.where(lane < 64, below, above), 64, 1)
        return c

    columns(0, 12, 6, ends, 0)
    fine_rho4 = sender.exchange(sender.group(), rho0, l0, 5, AROUND, (4, 5), zeros=zeros, cut=True)
    sender.exchange(fine_r, r0, l0, 4, CORNERS, cut=True)
    sender.exchange(fine_r, r0, l0, 4, FACES, (4, 5))

    restricted(rho0, rho1, l0, l1, 0.5)
    restricted(rho1, rho2, l1, l2, 0.5)
    density1 = sender.exchange(sender.group(), rho1, l1, 7, diamond(6, 7, 2), zeros=zeros)
    density2 = sender.exchange(sender.group(), rho2, l2, 8, line_y2, zeros=zeros)

    fine_rho.wait_recv()
    face_coefficients(rho0, co0, l0, 4, 4, (0, 4))
    fine_rho4.wait_recv()
    face_coefficients(rho0, co0, l0, 4, 5, (4, 5))
    other_coefficients(rho0, co0, l0, 4, 4)
    fine_r.wait_recv()
    fine_r.wait_send()
    begin(r0, co0[4], d01, l0, 4, first, 4)
    smooth(d01, r0, d02, co0, l0, 3, *pairs[0], 9)
    smooth(d02, r0, d03, co0, l0, 2, *pairs[1], 8)
    smooth(d03, r0, d04, co0, l0, 1, *pairs[2], 7)

    def finish_down0(i, ys, here, applied):
        up0[i, :, ys, :] = r0[i, :, ys, :] - applied
        x0[i, :, ys, :] = (d01[i, :, ys, :] + d02[i, :, ys, :]) + (d03[i, :, ys, :] + here)

    sweep(d04, co0, l0, 0, 6, finish_down0)

    restricted(up0, r1, l0, l1)
    second = sender.exchange(sender.group(), r1, l1, 4, AROUND)
    density2.wait_recv()
    density2x = sender.exchange(sender.group(), rho2, l2, 8, line_x2, whole_y=True, zeros=zeros)
    density1.wait_recv()
    density1.wait_send()
    coefficients(rho1, co1, l1, 6, 3)
    back0 = sender.exchange(sender.group(), up0, l0, 4, AROUND)
    second.wait_recv()
    second.wait_send()
    begin(r1, co1[4], d11, l1, 4, first, 7)
    smooth(d11, r1, d12, co1, l1, 3, *pairs[0], 12)
    smooth(d12, r1, d13, co1, l1, 2, *pairs[1], 10)
    smooth(d13, r1, d14, co1, l1, 1, *pairs[2], 8)

    def finish_down1(i, ys, here, applied):
        up1[i, :, ys, :] = r1[i, :, ys, :] - applied
        x1[i, :, ys, :] = (d11[i, :, ys, :] + d12[i, :, ys, :]) + (d13[i, :, ys, :] + here)

    sweep(d14, co1, l1, 0, 6, finish_down1)

    restricted(up1, r2, l1, l2)
    third = sender.exchange(sender.group(), r2, l2, 7, coarse_offsets)
    density2x.wait_recv()
    density2.wait_send()
    density2x.wait_send()
    coefficients(rho2, co2, l2, 7, 4)
    back1 = sender.exchange(sender.group(), up1, l1, 6, AROUND)
    sender.exchange(back1, x1, l1, 3, AROUND, zeros=zeros)
    third.wait_recv()
    third.wait_send()
    begin(r2, co2[4], d21, l2, 7, first2, 17)

    def copy_total(i, c):
        x2[i, :, l2["h"] : l2["h"] + 3, :] = d21[i, :, l2["h"] : l2["h"] + 3, :]
        return c

    columns(l2["h"], l2["h"] + 3, 3, copy_total, 0)
    v, d = d21, d22
    for k, (alpha, beta) in enumerate(pairs2):
        smooth(v, r2, d, co2, l2, 6 - k, alpha, beta, 15)
        v, d = d, v

        def add_total(i, c, v=v):
            x2[i, :, l2["h"] : l2["h"] + 3, :] = x2[i, :, l2["h"] : l2["h"] + 3, :] + v[i, :, l2["h"] : l2["h"] + 3, :]
            return c

        columns(l2["h"], l2["h"] + 3, 3, add_total, 0)

    fourth = sender.exchange(sender.group(), x2, l2, 4, diamond(3, 4, 2), zeros=zeros)
    back1.wait_recv()
    back1.wait_send()
    fourth.wait_recv()
    prolonged(x2, u1, l2, l1, 4)
    smooth(u1, up1, d11, co1, l1, 6, None, first, 9)
    smooth(d11, up1, d12, co1, l1, 5, *pairs[0], 8)
    smooth(d12, up1, d13, co1, l1, 4, *pairs[1], 14)
    alpha, beta = pairs[2]

    def finish_up1(i, ys, here, applied):
        new = alpha * here + beta * (co1[4][i, :, ys, :] * (up1[i, :, ys, :] - applied))
        total = (x1[i, :, ys, :] + u1[i, :, ys, :]) + (d11[i, :, ys, :] + d12[i, :, ys, :])
        x1[i, :, ys, :] = total + (here + new)

    sweep(d13, co1, l1, 3, 12, finish_up1)

    prolonged(x1, u0, l1, l0, 3)
    back0.wait_recv()
    back0.wait_send()
    smooth(u0, up0, d01, co0, l0, 4, None, first, 10)
    smooth(d01, up0, d02, co0, l0, 3, *pairs[0], 9)
    smooth(d02, up0, d03, co0, l0, 2, *pairs[1], 8)
    smooth(d03, up0, d04, co0, l0, 1, *pairs[2], 7)

    def finish_up0(i, ys, here, applied):
        j = i - l0["h"]
        total = (x0[i, :, ys, :] + u0[i, :, ys, :]) + (d01[i, :, ys, :] + d02[i, :, ys, :])
        total = total + (d03[i, :, ys, :] + here)
        rest = up0[i, :, ys, :] - applied
        for t in range(4):
            out[0, j, :, 128 * t : 128 * t + 128] = total[t]
            out[1, j, :, 128 * t : 128 * t + 128] = rest[t]

    sweep(d04, co0, l0, 0, 6, finish_up0)
    pl.when(has_above)(upwards.wait_send)
    pl.when(has_below)(downwards.wait_send)
    fine_rho.wait_send()
    fine_rho4.wait_send()
    fourth.wait_send()


GROUPS = 13


def per_device(sizes, right_side, phase):
    def field(level):
        return pltpu.VMEM((level["cols"], level["t"], level["rows"], 128), jnp.float32)

    l0, l1, l2 = LEVELS
    shape = right_side.shape
    result = pltpu.VMEM(shape, jnp.float32)
    whole = pl.BlockSpec(memory_space=pltpu.VMEM)
    both = pl.pallas_call(
        functools.partial(kernel, sizes),
        out_shape=pltpu.VMEM((2,) + shape, jnp.float32),
        in_specs=[pl.BlockSpec(memory_space=pl.ANY)] * 2,
        out_specs=whole,
        scratch_shapes=[field(l0)] * 14
        + [field(l1)] * 14
        + [field(l2)] * 10
        + [pltpu.VMEM(shape, jnp.int32)]
        + [pltpu.VMEM((12, 16, 128), jnp.float32)] * 4
        + [pltpu.VMEM((1280, 128), jnp.float32), pltpu.VMEM((12, 4, 24, 128), jnp.float32)]
        + [pltpu.SemaphoreType.DMA((5,))]
        + [pltpu.SemaphoreType.DMA((GROUPS,))] * 2,
        compiler_params=pltpu.CompilerParams(
            collective_id=0, has_side_effects=True, vmem_limit_bytes=56 * 1024 * 1024
        ),
        cost_estimate=pl.CostEstimate(flops=60_000_000, bytes_accessed=1_200_000, transcendentals=0),
        name="cycle",
    )(right_side, phase)
    return both[0], both[1]


def solution(mesh):
    spec = P("gx", "gy", "gz")
    return jax.shard_map(
        functools.partial(per_device, dict(mesh.shape)),
        mesh=mesh,
        in_specs=(spec, spec),
        out_specs=(spec, spec),
        check_vma=False,
    )
```
